512 devices in a mesh: chrom: 256 (over z_hi, x, y, core), chan: 2 (over z_lo).
Axes of the slice: x: 4, y: 8, z: 8 (z_hi: 4, z_lo: 2; z = z_hi * 2 + z_lo), core: 2. Of those that a mesh axis runs over, the one named last changes fastest.
Arguments:
- left_embed: bfloat16 [4096, 256], P('chrom', 'chan'), may hold values from -6 to 6
- right_embed: bfloat16 [4096, 256], P('chrom', 'chan'), may hold values from -6 to 6
- conv_weight: bfloat16 [3, 3, 3, 256, 256], P(None, None, None, None, 'chan'), may hold values from -0.125 to 0.125
- readout: float32 [256], P('chan'), may hold values from -0.375 to 0.375
- cotangent: float32 [4096, 64], P('chrom'), may hold values from -6 to 6
Outputs:
- contact: float32 [4096, 64], P('chrom')
- left_grad: float32 [4096, 256], P('chrom', 'chan')
- right_grad: float32 [4096, 256], P('chrom', 'chan')
The draws below stay inside these ranges and needn't reach their ends.
All inputs are finite; a program needn't handle non-finite values.
Results may differ from the reference program's by a relative error of at most 0.013.
Values may be sent and summed in bfloat16 or wider, within the bound.
No kernel may reach another device: no remote copies, remote signals or barrier semaphores. Data moves between devices by JAX's collectives and lax.ppermute only.
A program may use at most 64 MiB of HBM per device.

```python
import jax
import jax.numpy as jnp
from jax import lax

C = 256
WIN = 64
LAYERS = 3
L = 4096
N_CHAN = 2


def block_levels(key, shape, pieces, low, top_value):
    loudness = 1.0
    for position, shards_of in pieces:
        steps = jax.random.uniform(jax.random.fold_in(jax.random.fold_in(key, 6), position), (shards_of,), jnp.float32, low / len(pieces), top_value / len(pieces))
        loudness = loudness * jnp.repeat(jnp.exp(steps), shape[position] // shards_of).reshape((-1,) + (1,) * (len(shape) - 1 - position))
    return loudness


def noise(rng, shape, width, most, cuts=(), held_as=jnp.bfloat16):
    values = width * jax.random.normal(rng, shape, jnp.float32)
    if cuts:
        values = values * block_levels(rng, shape, cuts, -0.22, 0.18)
    return jnp.clip(values, -most, most).astype(held_as)


def setup_inputs(seed: int = 0) -> dict:
    splits = jax.random.split(jax.random.key(seed), 6)
    left_embed = noise(splits[0], (L, C), 1.0, 6.0, ((0, 256), (1, 2)))
    right_embed = noise(splits[1], (L, C), 1.0, 6.0, ((0, 256), (1, 2)))
    conv_weight = noise(splits[2], (LAYERS, 3, 3, C, C), (9 * C) ** -0.5, 0.125, ((4, 2),))
    readout = noise(splits[3], (C,), C ** -0.5, 0.375, ((0, 2),), jnp.float32)
    cotangent = noise(splits[4], (L, WIN), 1.0, 6.0, ((0, 256),), jnp.float32)
    return dict(left_embed=left_embed, right_embed=right_embed, conv_weight=conv_weight, readout=readout, cotangent=cotangent)


def silu_grad(z):
    s = jax.nn.sigmoid(z)
    return s * (1.0 + z * (1.0 - s))

def reference(left_embed, right_embed, conv_weight, readout, cotangent):
    total_bins = left_embed.shape[0]
    channels = left_embed.shape[1]
    share = channels // N_CHAN
    padded_right = jnp.concatenate([right_embed, jnp.zeros((WIN, channels), jnp.bfloat16)], axis=0)
    index = (jnp.arange(total_bins, dtype=jnp.int32)[:, None] + jnp.arange(WIN, dtype=jnp.int32)[None, :]).astype(jnp.int32)
    pair = (left_embed.astype(jnp.float32)[:, None, :] + padded_right[index].astype(jnp.float32)).astype(jnp.bfloat16)
    states = []
    for layer in range(LAYERS):
        r = 2 ** layer
        padded = jnp.pad(pair, ((r, r), (r, r), (0, 0)))
        pre = jnp.zeros((total_bins, WIN, channels), jnp.float32)
        for a in range(3):
            for b in range(3):
                piece = padded[a * r:a * r + total_bins, b * r:b * r + WIN, :].reshape(-1, channels)
                pre = pre + jnp.dot(piece, conv_weight[layer, a, b], preferred_element_type=jnp.float32).reshape(total_bins, WIN, channels)
        states.append(pre)
        pair = (pair.astype(jnp.float32) + jax.nn.silu(pre)).astype(jnp.bfloat16)
    contact = lax.optimization_barrier(jnp.sum(pair.astype(jnp.float32) * readout[None, None, :], axis=-1))
    grad = cotangent[:, :, None] * readout[None, None, :]
    for layer in reversed(range(LAYERS)):
        r = 2 ** layer
        dpre = (grad * silu_grad(states[layer])).astype(jnp.bfloat16)
        padded = jnp.pad(dpre, ((r, r), (r, r), (0, 0)))
        total = grad
        for group in range(N_CHAN):
            part = jnp.zeros((total_bins, WIN, channels), jnp.float32)
            for a in range(3):
                for b in range(3):
                    piece = padded[(2 - a) * r:(2 - a) * r + total_bins, (2 - b) * r:(2 - b) * r + WIN, group * share:(group + 1) * share].reshape(-1, share)
                    kernel = conv_weight[layer, a, b][:, group * share:(group + 1) * share]
                    part = part + jnp.dot(piece, kernel.T, preferred_element_type=jnp.float32).reshape(total_bins, WIN, channels)
            total = total + part.astype(jnp.bfloat16).astype(jnp.float32)
        grad = total
    left_grad = lax.optimization_barrier(jnp.sum(grad, axis=1))

    def add_diagonal(step, acc):
        column = lax.dynamic_index_in_dim(grad, step, 1, keepdims=False)
        start = step.astype(jnp.int32)
        current = lax.dynamic_slice_in_dim(acc, start, total_bins, 0)
        return lax.dynamic_update_slice_in_dim(acc, current + column, start, 0)
    accum = lax.fori_loop(0, WIN, add_diagonal, jnp.zeros((total_bins + WIN, channels), jnp.float32))
    right_grad = accum[:total_bins]
    return (contact, left_grad, right_grad)
```

```python
import jax
import jax.numpy as jnp
from jax import lax
from jax.experimental import pallas as pl
from jax.experimental.pallas import tpu as pltpu
from jax.sharding import Mesh, PartitionSpec as P

BF = jnp.bfloat16
F32 = jnp.float32
CHROM = ("h", "yh", "yl", "core")
GROUP = ("yl", "core", "chan")
ALL = CHROM + ("chan",)
BAND = 64
C = 256
HALF = 128
OWN = 8
NT = (((1,), (1,)), ((), ()))


def dot(x, y):
    return jnp.dot(x, y, preferred_element_type=F32)


def dot_nt(x, y):
    return lax.dot_general(x, y, NT, preferred_element_type=F32)


def shifted(x, by):
    n = x.shape[0]
    if by > 0:
        return jnp.concatenate([x[by:], jnp.zeros((by, x.shape[1]), x.dtype)], axis=0)
    return jnp.concatenate([jnp.zeros((-by, x.shape[1]), x.dtype), x[: n + by]], axis=0)


def put(ref, row, x, r, sign):
    ref[row, :, 0:C] = shifted(x, -sign * r).astype(BF)
    ref[row, :, C : 2 * C] = x.astype(BF)
    ref[row, :, 2 * C : 3 * C] = shifted(x, sign * r).astype(BF)


def silu_parts(z):
    h = 0.5 * z
    t = jnp.tanh(h)
    return t, h + h * t


def slope(t, silu):
    s = 0.5 + 0.5 * t
    return s + silu * (0.5 - 0.5 * t)


def body(
    info, msg, w_own, w_z, w_s, out,
    w, lcan, rcan, ccan, lwin, rwin, u_all, v_all, e0, e63,
    pp1, pp2, pd2, pd1, ds0, ds1, g2, p3, d0, g1h, g1l, rcv, lcv, ccv, sem,
):
    q, first, core, chan, total = info[0], info[1], info[2], info[3], info[4]
    mine = pl.ds(pl.multiple_of(chan * HALF, HALF), HALF)
    theirs = pl.ds(pl.multiple_of((1 - chan) * HALF, HALF), HALF)
    near = pl.ds(pl.multiple_of(core * HALF, HALF), HALF)
    far = pl.ds(pl.multiple_of((1 - core) * HALF, HALF), HALF)
    copies = []
    for k in range(3):
        taps = pl.ds(9 * k, 9)
        copies.append([
            pltpu.make_async_copy(w_own.at[taps], w.at[taps, :, mine], sem.at[k, 0]),
            pltpu.make_async_copy(w_z.at[taps], w.at[taps, near, theirs], sem.at[k, 1]),
            pltpu.make_async_copy(w_s.at[taps], w.at[taps, far, theirs], sem.at[k, 2]),
        ])
        for c in copies[k]:
            c.start()

    def valid(row):
        i = first + row
        return jnp.where((i >= 0) & (i < total), 1.0, 0.0).astype(F32)

    lcan[160:176] = jnp.zeros((16, C), F32)
    rcan[160:176] = jnp.zeros((16, C), F32)
    ccan[160:192] = jnp.zeros((32, HALF), F32)
    for j in range(4):
        for g in range(2):
            e = 2 * j + g
            lanes = slice(HALF * g, HALF * g + HALF)
            places = [(16, 16 + 16 * j), (64, 80 + 16 * j)]
            if j == 0:
                places.append((112, 0))
            if j == 3:
                places.append((112, 144))
            for at, to in places:
                lcan[to : to + 16, lanes] = msg[e, at : at + 16].astype(F32)
                rcan[to : to + 16, lanes] = msg[e, at + 16 : at + 32].astype(F32)
                cot = msg[e, at + 32 : at + 48].astype(F32)
                if g == 0:
                    ccan[to : to + 16] = cot
                else:
                    ccan[to : to + 16] = ccan[to : to + 16] + cot
    read3 = jnp.concatenate([msg[0, 0:16], msg[1, 0:16]], axis=1).astype(F32)
    readout = jnp.sum(read3, axis=0, keepdims=True)
    start = pl.multiple_of(q * OWN, OWN)
    lwin[...] = lcan[pl.ds(start, 48)]
    rwin[...] = rcan[pl.ds(start, 112)]
    cot_t = jnp.transpose(ccan[pl.ds(pl.multiple_of(start + 8, OWN), 128)])

    for c in copies[0]:
        c.wait()
    ul, va, vb = [None] * 3, [None] * 3, [None] * 3
    for b in range(3):
        for a in range(3):
            lhs = jnp.concatenate([lwin[2 + a : 42 + a], rwin[1 + a + b : 105 + a + b]], axis=0)
            y = dot(lhs.astype(BF), w[3 * a + b])
            ul[b] = y[:40] if a == 0 else ul[b] + y[:40]
            if a == 0:
                va[b] = y[40:]
            else:
                vb[b] = y[40:] if a == 1 else vb[b] + y[40:]
    u_all[...] = ul[0] + ul[1] + ul[2]
    for var in range(2):
        v = [vb[b] + va[b] if var == 0 else vb[b] for b in range(3)]
        v_all[var] = v[0] + v[1] + v[2]
        e0[var] = ul[1] + ul[2] + (v[1] + v[2])[:40]
        e63[var] = ul[0] + ul[1] + (v[0] + v[1])[63:103]
    diag = lax.broadcasted_iota(jnp.int32, (BAND, C), 0)
    for t in range(34):
        row = t - 13
        var = jnp.where(first + row == 0, 1, 0)
        pair = (lwin[t + 3 : t + 4] + rwin[t + 3 : t + 67]).astype(BF).astype(F32)
        pre = u_all[t : t + 1] + v_all[var, t : t + BAND]
        pre = jnp.where(diag == 0, e0[var, t : t + 1], pre)
        pre = jnp.where(diag == BAND - 1, e63[var, t : t + 1], pre)
        th, sil = silu_parts(pre)
        if 12 <= t < 22:
            ds0[t - 12] = slope(th, sil).astype(BF)
        put(pp1, t, (pair + sil) * valid(row), 2, 1)

    for c in copies[1]:
        c.wait()
    n = 5
    for t0 in range(0, 30, n):
        acc = None
        for a in range(3):
            x = pp1[t0 + 2 * a : t0 + 2 * a + n].reshape(n * BAND, 3 * C)
            y = dot(x, w[9 + 3 * a : 12 + 3 * a].reshape(3 * C, C))
            acc = y if acc is None else acc + y
        for s in range(n):
            t = t0 + s
            th, sil = silu_parts(acc[s * BAND : (s + 1) * BAND])
            if 8 <= t < 22:
                ds1[t - 8] = slope(th, sil).astype(BF)
            pair = pp1[t + 2, :, C : 2 * C].astype(F32)
            put(pp2, t, (pair + sil) * valid(t - 11), 4, 1)

    for c in copies[2]:
        c.wait()

    def top(row):
        return cot_t[:BAND, row + 8 : row + 9] * readout

    n = 11
    for t0 in range(0, 22, n):
        acc = None
        for a in range(3):
            x = pp2[t0 + 4 * a : t0 + 4 * a + n].reshape(n * BAND, 3 * C)
            y = dot(x, w[18 + 3 * a : 21 + 3 * a].reshape(3 * C, C))
            acc = y if acc is None else acc + y
        for s in range(n):
            t = t0 + s
            th, sil = silu_parts(acc[s * BAND : (s + 1) * BAND])
            if 7 <= t < 15:
                p3[t - 7] = (pp2[t + 4, :, C : 2 * C].astype(F32) + sil).astype(BF)
            put(pd2, t, top(t - 7) * slope(th, sil), 4, -1)
    ccv[...] = jnp.zeros((64, HALF), F32)
    read_b = read3.astype(BF)
    rows = [jnp.sum(dot_nt(read_b, p3[s]), axis=0, keepdims=True) for s in range(OWN)]
    ccv[pl.ds(start, OWN), :BAND] = jnp.concatenate(rows, axis=0)

    n = 7
    for t0 in range(0, 14, n):
        acc = None
        for a in range(3):
            x = pd2[t0 + 8 - 4 * a : t0 + 8 - 4 * a + n].reshape(n * BAND, 3 * C)
            for b in range(3):
                y = dot_nt(x[:, b * C : (b + 1) * C], w[18 + 3 * a + b])
                acc = y if acc is None else acc + y
        for s in range(n):
            t = t0 + s
            grad = top(t - 3) + acc[s * BAND : (s + 1) * BAND]
            if 2 <= t < 12:
                g2[t - 2] = grad
            put(pd1, t, grad * ds1[t].astype(F32) * valid(t - 3), 2, -1)

    n = 5
    for t0 in range(0, 10, n):
        acc = None
        for a in range(3):
            x = pd1[t0 + 4 - 2 * a : t0 + 4 - 2 * a + n].reshape(n * BAND, 3 * C)
            for b in range(3):
                y = dot_nt(x[:, b * C : (b + 1) * C], w[9 + 3 * a + b])
                acc = y if acc is None else acc + y
        for s in range(n):
            t = t0 + s
            grad = g2[t] + acc[s * BAND : (s + 1) * BAND]
            if 1 <= t < 9:
                hi = grad.astype(BF)
                g1h[t - 1] = hi
                g1l[t - 1] = (grad - hi.astype(F32)).astype(BF)
            d0[t] = (grad * ds0[t].astype(F32) * valid(t - 1)).astype(BF)

    def chooser(rows_in, a, b):
        shape = (80, rows_in * BAND)
        to = lax.broadcasted_iota(jnp.int32, shape, 0)
        at = lax.broadcasted_iota(jnp.int32, shape, 1)
        i = (at >> 6) + a
        d = (at & 63) + b
        inside = (i >= 0) & (i < OWN) & (d >= 0) & (d < BAND)
        hit = ((to < 72) & (i + d == to)) | ((to >= 72) & (i == to - 72))
        return jnp.where(inside & hit, 1.0, 0.0).astype(BF)

    own = chooser(OWN, 0, 0)
    total80 = dot(own, g1h[...].reshape(OWN * BAND, C)) + dot(own, g1l[...].reshape(OWN * BAND, C))
    dd = d0[...].reshape(10 * BAND, C)
    for a in range(3):
        for b in range(3):
            z = dot(chooser(10, a - 2, b - 1), dd)
            total80 = total80 + dot_nt(z.astype(BF), w[3 * a + b])
    rcv[...] = jnp.zeros((128, C), F32)
    lcv[...] = jnp.zeros((64, C), F32)
    rcv[pl.ds(start, 72)] = total80[:72]
    lcv[pl.ds(start, OWN)] = total80[72:]
    for j in range(4):
        for g in range(2):
            lanes = slice(HALF * g, HALF * g + HALF)
            out[2 * j + g, 0:16] = rcv[16 * j : 16 * j + 16, lanes]
            out[2 * j + g, 16:32] = rcv[64 + 16 * j : 80 + 16 * j, lanes]
            out[2 * j + g, 32:48] = lcv[16 * j : 16 * j + 16, lanes]
            out[2 * j + g, 48:64] = ccv[16 * j : 16 * j + 16]


def local_part(info, msg, w_own, w_z, w_s):
    vm = pltpu.VMEM
    scratch = [
        vm((27, C, C), BF),
        vm((176, C), F32),
        vm((176, C), F32),
        vm((192, HALF), F32),
        vm((48, C), F32),
        vm((112, C), F32),
        vm((40, C), F32),
        vm((2, 104, C), F32),
        vm((2, 40, C), F32),
        vm((2, 40, C), F32),
        vm((34, BAND, 3 * C), BF),
        vm((30, BAND, 3 * C), BF),
        vm((22, BAND, 3 * C), BF),
        vm((14, BAND, 3 * C), BF),
        vm((10, BAND, C), BF),
        vm((14, BAND, C), BF),
        vm((10, BAND, C), F32),
        vm((8, BAND, C), BF),
        vm((10, BAND, C), BF),
        vm((8, BAND, C), BF),
        vm((8, BAND, C), BF),
        vm((128, C), F32),
        vm((64, C), F32),
        vm((64, HALF), F32),
        pltpu.SemaphoreType.DMA((3, 3)),
    ]
    return pl.pallas_call(
        body,
        out_shape=jax.ShapeDtypeStruct((8, 64, HALF), F32),
        in_specs=[
            pl.BlockSpec(memory_space=pltpu.SMEM),
            pl.BlockSpec(memory_space=vm),
            pl.BlockSpec(memory_space=pl.ANY),
            pl.BlockSpec(memory_space=pl.ANY),
            pl.BlockSpec(memory_space=pl.ANY),
        ],
        out_specs=pl.BlockSpec(memory_space=vm),
        scratch_shapes=scratch,
        compiler_params=pltpu.CompilerParams(vmem_limit_bytes=48 * 2**20),
        cost_estimate=pl.CostEstimate(
            flops=6 * 10**9, bytes_accessed=5 * 10**6, transcendentals=2 * 10**6
        ),
        name="decoder",
    )(info, msg, w_own, w_z, w_s)


def flat(h, yh, yl, core, chan):
    return (((h * 4 + yh) * 2 + yl) * 2 + core) * 2 + chan


def z_pairs(chroms):
    pairs = []
    per_z = chroms // 4
    for ch in range(chroms):
        step = 1 if ch % 2 == 0 else -1
        hi, rest = ch // per_z, ch % per_z
        for g in range(2):
            z = (2 * hi + g + step) % 8
            pairs.append((((z // 2) * per_z + rest) * 2 + z % 2, 2 * ch + g))
    return pairs


def parts_of(x, count):
    parts = []
    for _ in range(count):
        hi = lax.reduce_precision(x, 8, 7)
        parts.append(hi.astype(BF))
        x = x - hi
    return parts


def local(left, right, weight, readout, cotangent):
    rows = left.shape[0]
    chroms = lax.axis_size(CHROM)
    slab = lax.axis_index(CHROM)
    core = lax.axis_index("core")
    chan = lax.axis_index("chan")
    own_w = weight.reshape(27, C, HALF)
    piece = lax.dynamic_slice_in_dim(own_w, core * HALF, HALF, axis=1)
    w_z = lax.ppermute(piece, ALL, z_pairs(chroms))

    hi, lo = parts_of(cotangent, 2)
    cot = jnp.pad(jnp.where(chan == 0, hi, lo), ((0, 0), (0, HALF - BAND)))
    mine = jnp.concatenate([left, right, cot], axis=0)
    slabs = 4
    groups = chroms // slabs
    next_group = [
        (slabs * (g + 1) + j, slabs * g + j) for g in range(groups - 1) for j in range(slabs)
    ]
    ends = [(slabs * g + 3, slabs * (g + 1)) for g in range(groups - 1)]
    ends += [(slabs * (g + 2), slabs * g + 3) for g in range(groups - 2)]
    after = lax.ppermute(mine, CHROM, next_group)
    edge = lax.ppermute(mine, CHROM, ends)
    read = jnp.pad(jnp.stack(parts_of(readout, 3)), ((0, 13), (0, 0)))
    block = jnp.concatenate([read, mine, after, edge], axis=0)
    msg = lax.all_to_all(
        jnp.broadcast_to(block[None], (8,) + block.shape), GROUP, 0, 0, tiled=False
    )
    w_s = lax.ppermute(w_z, "core", [(0, 1), (1, 0)])
    q = lax.axis_index(GROUP)
    info = jnp.stack(
        [q, rows * slab + OWN * chan, core, chan, rows * chroms]
    ).astype(jnp.int32)
    sent = local_part(info, msg, own_w, w_z, w_s)
    got = jnp.sum(lax.all_to_all(sent, GROUP, 0, 0, tiled=False), axis=0)
    moved = lax.ppermute(got[16:32], CHROM, [(b, a) for a, b in next_group])
    return got[48:64, :BAND], got[32:48], got[0:16] + moved


def solution(mesh):
    chroms = mesh.shape["chrom"]
    small = Mesh(
        mesh.devices.reshape(chroms // 16, 4, 2, 2, 2), ("h", "yh", "yl", "core", "chan")
    )
    return jax.shard_map(
        local,
        mesh=small,
        in_specs=(
            P(CHROM, "chan"),
            P(CHROM, "chan"),
            P(None, None, None, None, "chan"),
            P("chan"),
            P(CHROM, None),
        ),
        out_specs=(P(CHROM, None), P(CHROM, "chan"), P(CHROM, "chan")),
        check_vma=False,
    )
```

```python
import jax
import jax.numpy as jnp
from jax import lax
from jax.experimental import pallas as pl
from jax.experimental.pallas import tpu as pltpu
from jax.sharding import Mesh, PartitionSpec as P

BF = jnp.bfloat16
F32 = jnp.float32
CHROM = ("h", "yh", "yl", "core")
GROUP = ("yl", "core", "chan")
ALL = CHROM + ("chan",)
BAND = 64
C = 256
HALF = 128
OWN = 8
NT = (((1,), (1,)), ((), ()))


def dot(x, y):
    return jnp.dot(x, y, preferred_element_type=F32)


def dot_nt(x, y):
    return lax.dot_general(x, y, NT, preferred_element_type=F32)


def shifted(x, by):
    n = x.shape[0]
    if by > 0:
        return jnp.concatenate([x[by:], jnp.zeros((by, x.shape[1]), x.dtype)], axis=0)
    return jnp.concatenate([jnp.zeros((-by, x.shape[1]), x.dtype), x[: n + by]], axis=0)


def put(ref, row, x, r, sign):
    ref[row, :, 0:C] = shifted(x, -sign * r)
    ref[row, :, C : 2 * C] = x
    ref[row, :, 2 * C : 3 * C] = shifted(x, sign * r)


def gate(h):
    p = 1.0 + jnp.tanh(h)
    return p, h * p


def slope2(p, silu):
    return p + silu * (2.0 - p)


def spans(rows, n):
    return [(t, min(n, rows - t)) for t in range(0, rows, n)]


def side_by_side(w, tap):
    return jnp.concatenate([w[tap + k] for k in range(9)], axis=1)


def body(
    info, msg, w_own, w_z, w_s, out,
    w, lcan, rcan, ccan, lwin, rwin, u_all, v_all, e0, e63,
    pp1, pp2, pd2, pd1, ds0, ds1, g2, p3, d0, g1h, g1l, rcv, lcv, ccv, sem,
):
    q, first, core, chan, total = info[0], info[1], info[2], info[3], info[4]
    mine = pl.ds(pl.multiple_of(chan * HALF, HALF), HALF)
    theirs = pl.ds(pl.multiple_of((1 - chan) * HALF, HALF), HALF)
    near = pl.ds(core * 13, 14)
    far = pl.ds((1 - core) * 13, 14)
    first_copies = [
        pltpu.make_async_copy(w_z, w.at[near, :, theirs], sem.at[3]),
        pltpu.make_async_copy(w_s, w.at[far, :, theirs], sem.at[4]),
    ]
    copies = []
    for k in range(3):
        taps = pl.ds(9 * k, 9)
        copies.append(pltpu.make_async_copy(w_own.at[taps], w.at[taps, :, mine], sem.at[k]))
    first_copies.append(copies[0])
    for c in first_copies + copies[1:]:
        c.start()

    def valid(row):
        i = first + row
        return jnp.where((i >= 0) & (i < total), 1.0, 0.0)

    lcan[96:176] = jnp.zeros((80, C), F32)
    rcan[160:176] = jnp.zeros((16, C), F32)
    ccan[96:192] = jnp.zeros((96, HALF), F32)
    def place(ref, to, lanes, x):
        ref[to : to + 16, lanes] = x.astype(F32)

    for j in range(4):
        for g in range(2):
            e = 2 * j + g
            lanes = slice(HALF * g, HALF * g + HALF)
            place(lcan, 16 + 16 * j, lanes, msg[e, 0:16])
            place(rcan, 16 + 16 * j, lanes, msg[e, 16:32])
            place(rcan, 80 + 16 * j, lanes, msg[e, 48:64])
            if j == 0:
                place(lcan, 80, lanes, msg[e, 64:80])
            if j == 1:
                place(lcan, 0, lanes, msg[e, 64:80])
                place(rcan, 0, lanes, msg[e, 80:96])
            if j == 3:
                place(rcan, 144, lanes, msg[e, 80:96])
    for to, j, at in ((0, 1, 96), (16, 0, 32), (32, 1, 32), (48, 2, 32), (64, 3, 32), (80, 0, 96)):
        ccan[to : to + 16] = msg[2 * j, at : at + 16].astype(F32) + msg[2 * j + 1, at : at + 16].astype(F32)
    halves = []
    lane = lax.broadcasted_iota(jnp.int32, (1, HALF), 1)
    for g in range(2):
        m = msg[g, 32:48].astype(F32)
        even, odd = m[0:1] + m[2:3] + m[4:5], m[1:2] + m[3:4] + m[5:6]
        halves.append(jnp.where(lane < BAND, pltpu.roll(even, BAND, 1), odd))
    readout = jnp.concatenate(halves, axis=1)
    rest, parts = readout, []
    for _ in range(3):
        parts.append(rest.astype(BF).astype(F32))
        rest = rest - parts[-1]
    read_b = jnp.concatenate(parts + [jnp.zeros((13, C), F32)], axis=0).astype(BF)
    start = pl.multiple_of(q * OWN, OWN)
    lwin[...] = lcan[pl.ds(start, 48)]
    rwin[...] = rcan[pl.ds(start, 112)]
    cot_t = jnp.transpose(ccan[pl.ds(pl.multiple_of(start + 8, OWN), 128)])

    for c in first_copies:
        c.wait()
    ul, va, vb = [None] * 3, [None] * 3, [None] * 3
    for b in range(3):
        for a in range(3):
            lhs = jnp.concatenate([lwin[2 + a : 42 + a], rwin[1 + a + b : 105 + a + b]], axis=0)
            y = dot(lhs.astype(BF), w[3 * a + b])
            ul[b] = y[:40] if a == 0 else ul[b] + y[:40]
            if a == 0:
                va[b] = y[40:]
            else:
                vb[b] = y[40:] if a == 1 else vb[b] + y[40:]
    u_all[...] = ul[0] + ul[1] + ul[2]
    for var in range(2):
        v = [vb[b] + va[b] if var == 0 else vb[b] for b in range(3)]
        v_all[var] = v[0] + v[1] + v[2]
        e0[var] = ul[1] + ul[2] + (v[1] + v[2])[:40]
        e63[var] = ul[0] + ul[1] + (v[0] + v[1])[63:103]
    tile = lax.broadcasted_iota(jnp.int32, (8, C), 0)

    def row_0(t):
        row = t - 13
        var = jnp.where(first + row == 0, 1, 0)
        pair = (lwin[t + 3 : t + 4] + rwin[t + 3 : t + 67]).astype(BF).astype(F32)
        pre = u_all[t : t + 1] + v_all[var, t : t + BAND]
        pre = jnp.concatenate(
            [
                jnp.where(tile == 0, e0[var, t : t + 1], pre[:8]),
                pre[8 : BAND - 8],
                jnp.where(tile == 7, e63[var, t : t + 1], pre[BAND - 8 :]),
            ],
            axis=0,
        )
        p, sil = gate(0.5 * pre)
        if 12 <= t < 22:
            ds0[t - 12] = slope2(p, sil).astype(BF)
        put(pp1, t, ((pair + sil) * valid(row)).astype(BF), 2, 1)

    copies[1].wait()
    done = 0
    for t0, n in spans(30, 3):
        while done < t0 + n + 4:
            row_0(done)
            done += 1
        x = [pp1[t0 + 2 * a : t0 + 2 * a + n].reshape(n * BAND, 3 * C) for a in range(3)]
        acc = dot(jnp.concatenate(x, axis=1), w[9:18].reshape(9 * C, C))
        for s in range(n):
            t = t0 + s
            p, sil = gate(0.5 * acc[s * BAND : (s + 1) * BAND])
            if 8 <= t < 22:
                ds1[t - 8] = slope2(p, sil).astype(BF)
            pair = pp1[t + 2, :, C : 2 * C].astype(F32)
            put(pp2, t, ((pair + sil) * valid(t - 11)).astype(BF), 4, 1)

    copies[2].wait()

    half = 0.5 * readout

    def top(row, scale):
        return cot_t[:BAND, row + 8 : row + 9] * scale

    for t0, n in spans(22, 4):
        x = [pp2[t0 + 4 * a : t0 + 4 * a + n].reshape(n * BAND, 3 * C) for a in range(3)]
        acc = dot(jnp.concatenate(x, axis=1), w[18:27].reshape(9 * C, C))
        for s in range(n):
            t = t0 + s
            p, sil = gate(0.5 * acc[s * BAND : (s + 1) * BAND])
            if 7 <= t < 15:
                p3[t - 7] = (pp2[t + 4, :, C : 2 * C].astype(F32) + sil).astype(BF)
            put(pd2, t, (top(t - 7, half) * slope2(p, sil)).astype(BF), 4, -1)
    ccv[...] = jnp.zeros((64, HALF), F32)
    rows = [jnp.sum(dot_nt(read_b, p3[s]), axis=0, keepdims=True) for s in range(OWN)]
    ccv[pl.ds(start, OWN), :BAND] = jnp.concatenate(rows, axis=0)

    for t0, n in spans(14, 5):
        x = [pd2[t0 + 8 - 4 * a : t0 + 8 - 4 * a + n].reshape(n * BAND, 3 * C) for a in range(3)]
        acc = dot_nt(jnp.concatenate(x, axis=1), side_by_side(w, 18))
        for s in range(n):
            t = t0 + s
            grad = top(t - 3, readout) + acc[s * BAND : (s + 1) * BAND]
            if 2 <= t < 12:
                g2[t - 2] = grad
            put(pd1, t, (grad * ds1[t].astype(F32) * (0.5 * valid(t - 3))).astype(BF), 2, -1)

    for t0, n in spans(10, 5):
        x = [pd1[t0 + 4 - 2 * a : t0 + 4 - 2 * a + n].reshape(n * BAND, 3 * C) for a in range(3)]
        acc = dot_nt(jnp.concatenate(x, axis=1), side_by_side(w, 9))
        for s in range(n):
            t = t0 + s
            grad = g2[t] + acc[s * BAND : (s + 1) * BAND]
            if 1 <= t < 9:
                hi = grad.astype(BF)
                g1h[t - 1] = hi
                g1l[t - 1] = (grad - hi.astype(F32)).astype(BF)
            d0[t] = (grad * ds0[t].astype(F32) * (0.5 * valid(t - 1))).astype(BF)

    def iotas(shape):
        at = lax.broadcasted_iota(jnp.int32, shape, 1)
        return lax.broadcasted_iota(jnp.int32, shape, 0), at >> 6, at & 63

    def ones(hit):
        return jnp.where(hit, 1.0, 0.0).astype(BF)

    to, i, d = iotas((80, 10 * BAND))
    key = to - i - d
    along = {s: ones(key == s) for s in range(-3, 2)}
    to, i, d = iotas((16, 10 * BAND))
    key = jnp.where(to < OWN, to - i, 99)
    across = [ones(key == a - 2) for a in range(3)]
    unused, i, d = iotas((1, 10 * BAND))
    in_d = [ones((d >= 1 - b) & (d < BAND + 1 - b)) for b in range(3)]
    in_i = [ones((i >= 2 - a) & (i < OWN + 2 - a)) for a in range(3)]
    picks = []
    for a in range(3):
        for b in range(3):
            picks.append(along[a + b - 3] * (in_i[a] * in_d[b]))
            picks.append(across[a] * in_d[b])
    z = dot(jnp.concatenate(picks, axis=0), d0[...].reshape(10 * BAND, C)).astype(BF)
    z = jnp.concatenate([z[96 * k : 96 * k + 96] for k in range(9)], axis=1)
    own = jnp.concatenate([along[-1][:, BAND : 9 * BAND], across[1][:, BAND : 9 * BAND]], axis=0)
    top96 = dot(own, g1h[...].reshape(OWN * BAND, C)) + dot(own, g1l[...].reshape(OWN * BAND, C))
    top96 = top96 + dot_nt(z, side_by_side(w, 0))
    rcv[...] = jnp.zeros((128, C), F32)
    lcv[...] = jnp.zeros((64, C), F32)
    rcv[pl.ds(start, 72)] = top96[:72]
    lcv[pl.ds(start, OWN)] = top96[80:88]
    for j in range(4):
        for g in range(2):
            lanes = slice(HALF * g, HALF * g + HALF)
            out[2 * j + g, 0:16] = rcv[16 * j : 16 * j + 16, lanes]
            out[2 * j + g, 16:32] = rcv[64 + 16 * j : 80 + 16 * j, lanes]
            out[2 * j + g, 32:48] = lcv[16 * j : 16 * j + 16, lanes]
            out[2 * j + g, 48:64] = ccv[16 * j : 16 * j + 16]


def local_part(info, msg, w_own, w_z, w_s):
    vm = pltpu.VMEM
    scratch = [
        vm((27, C, C), BF),
        vm((176, C), F32),
        vm((176, C), F32),
        vm((192, HALF), F32),
        vm((48, C), F32),
        vm((112, C), F32),
        vm((40, C), F32),
        vm((2, 104, C), F32),
        vm((2, 40, C), F32),
        vm((2, 40, C), F32),
        vm((34, BAND, 3 * C), BF),
        vm((30, BAND, 3 * C), BF),
        vm((22, BAND, 3 * C), BF),
        vm((14, BAND, 3 * C), BF),
        vm((10, BAND, C), BF),
        vm((14, BAND, C), BF),
        vm((10, BAND, C), F32),
        vm((8, BAND, C), BF),
        vm((10, BAND, C), BF),
        vm((8, BAND, C), BF),
        vm((8, BAND, C), BF),
        vm((128, C), F32),
        vm((64, C), F32),
        vm((64, HALF), F32),
        pltpu.SemaphoreType.DMA((5,)),
    ]
    return pl.pallas_call(
        body,
        out_shape=jax.ShapeDtypeStruct((8, 64, HALF), F32),
        in_specs=[
            pl.BlockSpec(memory_space=pltpu.SMEM),
            pl.BlockSpec(memory_space=vm),
            pl.BlockSpec(memory_space=pl.ANY),
            pl.BlockSpec(memory_space=pl.ANY),
            pl.BlockSpec(memory_space=pl.ANY),
        ],
        out_specs=pl.BlockSpec(memory_space=vm),
        scratch_shapes=scratch,
        compiler_params=pltpu.CompilerParams(vmem_limit_bytes=48 * 2**20),
        cost_estimate=pl.CostEstimate(
            flops=6 * 10**9, bytes_accessed=5 * 10**6, transcendentals=2 * 10**6
        ),
        name="decoder",
    )(info, msg, w_own, w_z, w_s)


def z_pairs(chroms):
    pairs = []
    per_z = chroms // 4
    for ch in range(chroms):
        hi, rest = ch // per_z, ch % per_z
        for g in range(2):
            step = (1 if g == 0 else -1) * (1 if ch % 2 == 0 else -1)
            z = (2 * hi + g + step) % 8
            pairs.append((((z // 2) * per_z + rest) * 2 + z % 2, 2 * ch + g))
    return pairs


def parts_of(x, count):
    parts = []
    for _ in range(count):
        hi = lax.reduce_precision(x, 8, 7)
        parts.append(hi.astype(BF))
        x = x - hi
    return parts


def local(left, right, weight, readout, cotangent):
    rows = left.shape[0]
    chroms = lax.axis_size(CHROM)
    slab = lax.axis_index(CHROM)
    core = lax.axis_index("core")
    chan = lax.axis_index("chan")
    own_w = weight.reshape(27, C, HALF)
    piece = jnp.where(core == 0, own_w[:14], own_w[13:])

    hi, lo = parts_of(cotangent, 2)
    read = jnp.pad(jnp.stack(parts_of(readout, 3)).reshape(6, BAND), ((0, rows - 6), (0, 0)))
    cot = jnp.concatenate([jnp.where(chan == 0, hi, lo), read], axis=1)
    mine = jnp.concatenate([left, right, cot], axis=0)
    piece, mine = lax.optimization_barrier((piece, mine))
    w_z = lax.ppermute(piece, "chan", [(0, 1), (1, 0)])
    slabs = 4
    groups = chroms // slabs
    next_group = [
        (slabs * (g + 1) + j, slabs * g + j) for g in range(groups - 1) for j in range(slabs)
    ]
    ends = [(slabs * g + 3, slabs * (g + 1) + 1) for g in range(groups - 1)]
    ends += [(slabs * (g + 2), slabs * g + 3) for g in range(groups - 2)]
    after = lax.ppermute(mine, CHROM, next_group)
    edge = lax.ppermute(mine, CHROM, ends)
    extra = jnp.where(slab % slabs == 0, after, edge)
    block = jnp.concatenate([mine, after[rows : 2 * rows], extra], axis=0)
    msg = lax.all_to_all(
        jnp.broadcast_to(block[None], (8,) + block.shape), GROUP, 0, 0, tiled=False
    )
    msg, w_z = lax.optimization_barrier((msg, w_z))
    w_s = lax.ppermute(w_z, "core", [(0, 1), (1, 0)])
    q = lax.axis_index(GROUP)
    info = jnp.stack(
        [q, rows * slab + OWN * chan, core, chan, rows * chroms]
    ).astype(jnp.int32)
    sent = local_part(info, msg, own_w, w_z, w_s)
    got = jnp.sum(lax.all_to_all(sent, GROUP, 0, 0, tiled=False), axis=0)
    moved = lax.ppermute(got[16:32], CHROM, [(b, a) for a, b in next_group])
    return got[48:64, :BAND], got[32:48], got[0:16] + moved


def solution(mesh):
    chroms = mesh.shape["chrom"]
    small = Mesh(
        mesh.devices.reshape(chroms // 16, 4, 2, 2, 2), ("h", "yh", "yl", "core", "chan")
    )
    return jax.shard_map(
        local,
        mesh=small,
        in_specs=(
            P(CHROM, "chan"),
            P(CHROM, "chan"),
            P(None, None, None, None, "chan"),
            P("chan"),
            P(CHROM, None),
        ),
        out_specs=(P(CHROM, None), P(CHROM, "chan"), P(CHROM, "chan")),
        check_vma=False,
    )
```

```python
import jax
import jax.numpy as jnp
from jax import lax
from jax.experimental import pallas as pl
from jax.experimental.pallas import tpu as pltpu
from jax.sharding import Mesh, PartitionSpec as P

BF = jnp.bfloat16
F32 = jnp.float32
CHROM = ("h", "yh", "yl", "core")
GROUP = ("yl", "core", "chan")
ALL = CHROM + ("chan",)
BAND = 64
C = 256
HALF = 128
OWN = 8
NT = (((1,), (1,)), ((), ()))


def dot(x, y):
    return jnp.dot(x, y, preferred_element_type=F32)


def dot_nt(x, y):
    return lax.dot_general(x, y, NT, preferred_element_type=F32)


def shifted(x, by):
    n = x.shape[0]
    if by > 0:
        return jnp.concatenate([x[by:], jnp.zeros((by, x.shape[1]), x.dtype)], axis=0)
    return jnp.concatenate([jnp.zeros((-by, x.shape[1]), x.dtype), x[: n + by]], axis=0)


def put(ref, row, x, r, sign):
    ref[row, :, 0:C] = shifted(x, -sign * r)
    ref[row, :, C : 2 * C] = x
    ref[row, :, 2 * C : 3 * C] = shifted(x, sign * r)


def gate(h):
    p = 1.0 + jnp.tanh(h)
    return p, h * p


def slope2(p, silu):
    return p + silu * (2.0 - p)


def spans(rows, n):
    return [(t, min(n, rows - t)) for t in range(0, rows, n)]


def side_by_side(w, tap):
    return jnp.concatenate([w[tap + k] for k in range(9)], axis=1)


def body(
    info, msg, w_own, w_z, w_s, out,
    w, lcan, rcan, ccan, lwin, rwin, u_all, v_all, e0, e63,
    pp1, pp2, pd2, pd1, ds0, ds1, g2, p3, d0, g1h, g1l, rcv, lcv, ccv, sem,
):
    q, first, core, chan, total = info[0], info[1], info[2], info[3], info[4]
    mine = pl.ds(pl.multiple_of(chan * HALF, HALF), HALF)
    theirs = pl.ds(pl.multiple_of((1 - chan) * HALF, HALF), HALF)
    near = pl.ds(core * 13, 14)
    far = pl.ds((1 - core) * 13, 14)
    first_copies = [
        pltpu.make_async_copy(w_z, w.at[near, :, theirs], sem.at[3]),
        pltpu.make_async_copy(w_s, w.at[far, :, theirs], sem.at[4]),
    ]
    copies = []
    for k in range(3):
        taps = pl.ds(9 * k, 9)
        copies.append(pltpu.make_async_copy(w_own.at[taps], w.at[taps, :, mine], sem.at[k]))
    first_copies.append(copies[0])
    for c in first_copies + copies[1:]:
        c.start()

    def valid(row):
        i = first + row
        return jnp.where((i >= 0) & (i < total), 1.0, 0.0)

    lcan[96:176] = jnp.zeros((80, C), F32)
    rcan[160:176] = jnp.zeros((16, C), F32)
    ccan[96:192] = jnp.zeros((96, HALF), F32)
    def place(ref, to, lanes, x):
        ref[to : to + 16, lanes] = x.astype(F32)

    for j in range(4):
        for g in range(2):
            e = 2 * j + g
            lanes = slice(HALF * g, HALF * g + HALF)
            place(lcan, 16 + 16 * j, lanes, msg[e, 0:16])
            place(rcan, 16 + 16 * j, lanes, msg[e, 16:32])
            place(rcan, 80 + 16 * j, lanes, msg[e, 48:64])
            if j == 0:
                place(lcan, 80, lanes, msg[e, 64:80])
            if j == 1:
                place(lcan, 0, lanes, msg[e, 64:80])
                place(rcan, 0, lanes, msg[e, 80:96])
            if j == 3:
                place(rcan, 144, lanes, msg[e, 80:96])
    for to, j, at in ((0, 1, 96), (16, 0, 32), (32, 1, 32), (48, 2, 32), (64, 3, 32), (80, 0, 96)):
        ccan[to : to + 16] = msg[2 * j, at : at + 16].astype(F32) + msg[2 * j + 1, at : at + 16].astype(F32)
    halves = []
    lane = lax.broadcasted_iota(jnp.int32, (1, HALF), 1)
    for g in range(2):
        m = msg[g, 32:48].astype(F32)
        even, odd = m[0:1] + m[2:3] + m[4:5], m[1:2] + m[3:4] + m[5:6]
        halves.append(jnp.where(lane < BAND, pltpu.roll(even, BAND, 1), odd))
    readout = jnp.concatenate(halves, axis=1)
    rest, parts = readout, []
    for _ in range(3):
        parts.append(rest.astype(BF).astype(F32))
        rest = rest - parts[-1]
    read_b = jnp.concatenate(parts + [jnp.zeros((13, C), F32)], axis=0).astype(BF)
    start = pl.multiple_of(q * OWN, OWN)
    lwin[...] = lcan[pl.ds(start, 48)]
    rwin[...] = rcan[pl.ds(start, 112)]
    cot_t = jnp.transpose(ccan[pl.ds(pl.multiple_of(start + 8, OWN), 128)])

    for c in first_copies:
        c.wait()
    ul, va, vb = [None] * 3, [None] * 3, [None] * 3
    for b in range(3):
        for a in range(3):
            lhs = jnp.concatenate([lwin[2 + a : 42 + a], rwin[1 + a + b : 105 + a + b]], axis=0)
            y = dot(lhs.astype(BF), w[3 * a + b])
            ul[b] = y[:40] if a == 0 else ul[b] + y[:40]
            if a == 0:
                va[b] = y[40:]
            else:
                vb[b] = y[40:] if a == 1 else vb[b] + y[40:]
    u_all[...] = ul[0] + ul[1] + ul[2]
    for var in range(2):
        v = [vb[b] + va[b] if var == 0 else vb[b] for b in range(3)]
        v_all[var] = v[0] + v[1] + v[2]
        e0[var] = ul[1] + ul[2] + (v[1] + v[2])[:40]
        e63[var] = ul[0] + ul[1] + (v[0] + v[1])[63:103]
    tile = lax.broadcasted_iota(jnp.int32, (8, C), 0)

    def row_0(t):
        row = t - 13
        var = jnp.where(first + row == 0, 1, 0)
        pair = (lwin[t + 3 : t + 4] + rwin[t + 3 : t + 67]).astype(BF).astype(F32)
        pre = u_all[t : t + 1] + v_all[var, t : t + BAND]
        pre = jnp.concatenate(
            [
                jnp.where(tile == 0, e0[var, t : t + 1], pre[:8]),
                pre[8 : BAND - 8],
                jnp.where(tile == 7, e63[var, t : t + 1], pre[BAND - 8 :]),
            ],
            axis=0,
        )
        p, sil = gate(0.5 * pre)
        if 12 <= t < 22:
            ds0[t - 12] = slope2(p, sil).astype(BF)
        put(pp1, t, ((pair + sil) * valid(row)).astype(BF), 2, 1)

    copies[1].wait()
    done = 0
    for t0, n in spans(30, 3):
        while done < t0 + n + 4:
            row_0(done)
            done += 1
        x = [pp1[t0 + 2 * a : t0 + 2 * a + n].reshape(n * BAND, 3 * C) for a in range(3)]
        acc = dot(jnp.concatenate(x, axis=1), w[9:18].reshape(9 * C, C))
        for s in range(n):
            t = t0 + s
            p, sil = gate(0.5 * acc[s * BAND : (s + 1) * BAND])
            if 8 <= t < 22:
                ds1[t - 8] = slope2(p, sil).astype(BF)
            pair = pp1[t + 2, :, C : 2 * C].astype(F32)
            put(pp2, t, ((pair + sil) * valid(t - 11)).astype(BF), 4, 1)

    copies[2].wait()

    half = 0.5 * readout

    def top(row, scale):
        return cot_t[:BAND, row + 8 : row + 9] * scale

    for t0, n in spans(22, 4):
        x = [pp2[t0 + 4 * a : t0 + 4 * a + n].reshape(n * BAND, 3 * C) for a in range(3)]
        acc = dot(jnp.concatenate(x, axis=1), w[18:27].reshape(9 * C, C))
        for s in range(n):
            t = t0 + s
            p, sil = gate(0.5 * acc[s * BAND : (s + 1) * BAND])
            if 7 <= t < 15:
                p3[t - 7] = (pp2[t + 4, :, C : 2 * C].astype(F32) + sil).astype(BF)
            put(pd2, t, (top(t - 7, half) * slope2(p, sil)).astype(BF), 4, -1)
    ccv[...] = jnp.zeros((64, HALF), F32)
    rows = [jnp.sum(dot_nt(read_b, p3[s]), axis=0, keepdims=True) for s in range(OWN)]
    contact = jnp.concatenate(rows, axis=0)
    hi = contact.astype(BF).astype(F32)
    ccv[pl.ds(start, OWN)] = jnp.concatenate([hi, contact - hi], axis=1)

    for t0, n in spans(14, 5):
        x = [pd2[t0 + 8 - 4 * a : t0 + 8 - 4 * a + n].reshape(n * BAND, 3 * C) for a in range(3)]
        acc = dot_nt(jnp.concatenate(x, axis=1), side_by_side(w, 18))
        for s in range(n):
            t = t0 + s
            grad = top(t - 3, readout) + acc[s * BAND : (s + 1) * BAND]
            if 2 <= t < 12:
                g2[t - 2] = grad
            put(pd1, t, (grad * ds1[t].astype(F32) * (0.5 * valid(t - 3))).astype(BF), 2, -1)

    for t0, n in spans(10, 5):
        x = [pd1[t0 + 4 - 2 * a : t0 + 4 - 2 * a + n].reshape(n * BAND, 3 * C) for a in range(3)]
        acc = dot_nt(jnp.concatenate(x, axis=1), side_by_side(w, 9))
        for s in range(n):
            t = t0 + s
            grad = g2[t] + acc[s * BAND : (s + 1) * BAND]
            if 1 <= t < 9:
                hi = grad.astype(BF)
                g1h[t - 1] = hi
                g1l[t - 1] = (grad - hi.astype(F32)).astype(BF)
            d0[t] = (grad * ds0[t].astype(F32) * (0.5 * valid(t - 1))).astype(BF)

    def iotas(shape):
        at = lax.broadcasted_iota(jnp.int32, shape, 1)
        return lax.broadcasted_iota(jnp.int32, shape, 0), at >> 6, at & 63

    def ones(hit):
        return jnp.where(hit, 1.0, 0.0).astype(BF)

    to, i, d = iotas((80, 10 * BAND))
    key = to - i - d
    along = {s: ones(key == s) for s in range(-3, 2)}
    to, i, d = iotas((16, 10 * BAND))
    key = jnp.where(to < OWN, to - i, 99)
    across = [ones(key == a - 2) for a in range(3)]
    unused, i, d = iotas((1, 10 * BAND))
    in_d = [ones((d >= 1 - b) & (d < BAND + 1 - b)) for b in range(3)]
    in_i = [ones((i >= 2 - a) & (i < OWN + 2 - a)) for a in range(3)]
    picks = []
    for a in range(3):
        for b in range(3):
            picks.append(along[a + b - 3] * (in_i[a] * in_d[b]))
            picks.append(across[a] * in_d[b])
    z = dot(jnp.concatenate(picks, axis=0), d0[...].reshape(10 * BAND, C)).astype(BF)
    z = jnp.concatenate([z[96 * k : 96 * k + 96] for k in range(9)], axis=1)
    own = jnp.concatenate([along[-1][:, BAND : 9 * BAND], across[1][:, BAND : 9 * BAND]], axis=0)
    top96 = dot(own, g1h[...].reshape(OWN * BAND, C)) + dot(own, g1l[...].reshape(OWN * BAND, C))
    top96 = top96 + dot_nt(z, side_by_side(w, 0))
    rcv[...] = jnp.zeros((128, C), F32)
    lcv[...] = jnp.zeros((64, C), F32)
    rcv[pl.ds(start, 72)] = top96[:72]
    lcv[pl.ds(start, OWN)] = top96[80:88]
    for j in range(4):
        for g in range(2):
            lanes = slice(HALF * g, HALF * g + HALF)
            out[2 * j + g, 0:16] = rcv[16 * j : 16 * j + 16, lanes].astype(BF)
            out[2 * j + g, 16:32] = rcv[64 + 16 * j : 80 + 16 * j, lanes].astype(BF)
            out[2 * j + g, 32:48] = lcv[16 * j : 16 * j + 16, lanes].astype(BF)
            out[2 * j + g, 48:64] = ccv[16 * j : 16 * j + 16].astype(BF)


def local_part(info, msg, w_own, w_z, w_s):
    vm = pltpu.VMEM
    scratch = [
        vm((27, C, C), BF),
        vm((176, C), F32),
        vm((176, C), F32),
        vm((192, HALF), F32),
        vm((48, C), F32),
        vm((112, C), F32),
        vm((40, C), F32),
        vm((2, 104, C), F32),
        vm((2, 40, C), F32),
        vm((2, 40, C), F32),
        vm((34, BAND, 3 * C), BF),
        vm((30, BAND, 3 * C), BF),
        vm((22, BAND, 3 * C), BF),
        vm((14, BAND, 3 * C), BF),
        vm((10, BAND, C), BF),
        vm((14, BAND, C), BF),
        vm((10, BAND, C), F32),
        vm((8, BAND, C), BF),
        vm((10, BAND, C), BF),
        vm((8, BAND, C), BF),
        vm((8, BAND, C), BF),
        vm((128, C), F32),
        vm((64, C), F32),
        vm((64, HALF), F32),
        pltpu.SemaphoreType.DMA((5,)),
    ]
    return pl.pallas_call(
        body,
        out_shape=jax.ShapeDtypeStruct((8, 64, HALF), BF),
        in_specs=[
            pl.BlockSpec(memory_space=pltpu.SMEM),
            pl.BlockSpec(memory_space=vm),
            pl.BlockSpec(memory_space=pl.ANY),
            pl.BlockSpec(memory_space=pl.ANY),
            pl.BlockSpec(memory_space=pl.ANY),
        ],
        out_specs=pl.BlockSpec(memory_space=vm),
        scratch_shapes=scratch,
        compiler_params=pltpu.CompilerParams(vmem_limit_bytes=48 * 2**20),
        cost_estimate=pl.CostEstimate(
            flops=6 * 10**9, bytes_accessed=5 * 10**6, transcendentals=2 * 10**6
        ),
        name="decoder",
    )(info, msg, w_own, w_z, w_s)


def z_pairs(chroms):
    pairs = []
    per_z = chroms // 4
    for ch in range(chroms):
        hi, rest = ch // per_z, ch % per_z
        for g in range(2):
            step = (1 if g == 0 else -1) * (1 if ch % 2 == 0 else -1)
            z = (2 * hi + g + step) % 8
            pairs.append((((z // 2) * per_z + rest) * 2 + z % 2, 2 * ch + g))
    return pairs


def copy_taps(core, w_own, out, sem):
    moves = [
        pltpu.make_async_copy(
            w_own.at[pl.ds(core[0] * 13 + 2 * k, 2)], out.at[pl.ds(2 * k, 2)], sem.at[k]
        )
        for k in range(7)
    ]
    for move in moves:
        move.start()
    for move in moves:
        move.wait()


def own_taps(core, w_own):
    return pl.pallas_call(
        copy_taps,
        out_shape=jax.ShapeDtypeStruct((14, C, HALF), BF),
        in_specs=[pl.BlockSpec(memory_space=pltpu.SMEM), pl.BlockSpec(memory_space=pl.ANY)],
        out_specs=pl.BlockSpec(memory_space=pltpu.VMEM),
        scratch_shapes=[pltpu.SemaphoreType.DMA((7,))],
        cost_estimate=pl.CostEstimate(flops=0, bytes_accessed=2 * 10**6, transcendentals=0),
        name="own_taps",
    )(core, w_own)


def parts_of(x, count):
    parts = []
    for _ in range(count):
        hi = lax.reduce_precision(x, 8, 7)
        parts.append(hi.astype(BF))
        x = x - hi
    return parts


def local(left, right, weight, readout, cotangent):
    rows = left.shape[0]
    chroms = lax.axis_size(CHROM)
    slab = lax.axis_index(CHROM)
    core = lax.axis_index("core")
    chan = lax.axis_index("chan")
    own_w = weight.reshape(27, C, HALF)
    piece = own_taps(core[None].astype(jnp.int32), own_w)
    piece, readout, cotangent = lax.optimization_barrier((piece, readout, cotangent))

    hi, lo = parts_of(cotangent, 2)
    read = jnp.pad(jnp.stack(parts_of(readout, 3)).reshape(6, BAND), ((0, rows - 6), (0, 0)))
    cot = jnp.concatenate([jnp.where(chan == 0, hi, lo), read], axis=1)
    mine = jnp.concatenate([left, right, cot], axis=0)
    piece, mine = lax.optimization_barrier((piece, mine))
    w_z = lax.ppermute(piece, "chan", [(0, 1), (1, 0)])
    slabs = 4
    groups = chroms // slabs
    next_group = [
        (slabs * (g + 1) + j, slabs * g + j) for g in range(groups - 1) for j in range(slabs)
    ]
    ends = [(slabs * g + 3, slabs * (g + 1) + 1) for g in range(groups - 1)]
    ends += [(slabs * (g + 2), slabs * g + 3) for g in range(groups - 2)]
    after = lax.ppermute(mine, CHROM, next_group)
    edge = lax.ppermute(mine, CHROM, ends)
    extra = jnp.where(slab % slabs == 0, after, edge)
    block = jnp.concatenate([mine, after[rows : 2 * rows], extra], axis=0)
    msg = lax.all_to_all(
        jnp.broadcast_to(block[None], (8,) + block.shape), GROUP, 0, 0, tiled=False
    )
    msg, w_z = lax.optimization_barrier((msg, w_z))
    w_s = lax.ppermute(w_z, "core", [(0, 1), (1, 0)])
    q = lax.axis_index(GROUP)
    info = jnp.stack(
        [q, rows * slab + OWN * chan, core, chan, rows * chroms]
    ).astype(jnp.int32)
    sent = local_part(info, msg, own_w, w_z, w_s)
    got = jnp.sum(lax.all_to_all(sent, GROUP, 0, 0, tiled=False).astype(F32), axis=0)
    moved = lax.ppermute(got[16:32], CHROM, [(b, a) for a, b in next_group])
    return got[48:64, :BAND] + got[48:64, BAND:], got[32:48], got[0:16] + moved


def solution(mesh):
    chroms = mesh.shape["chrom"]
    small = Mesh(
        mesh.devices.reshape(chroms // 16, 4, 2, 2, 2), ("h", "yh", "yl", "core", "chan")
    )
    return jax.shard_map(
        local,
        mesh=small,
        in_specs=(
            P(CHROM, "chan"),
            P(CHROM, "chan"),
            P(None, None, None, None, "chan"),
            P("chan"),
            P(CHROM, None),
        ),
        out_specs=(P(CHROM, None), P(CHROM, "chan"), P(CHROM, "chan")),
        check_vma=False,
    )
```

```python
import jax
import jax.numpy as jnp
from jax import lax
from jax.experimental import pallas as pl
from jax.experimental.pallas import tpu as pltpu
from jax.sharding import Mesh, PartitionSpec as P

BF = jnp.bfloat16
F32 = jnp.float32
CHROM = ("h", "yh", "yl", "core")
GROUP = ("yl", "core", "chan")
ALL = CHROM + ("chan",)
BAND = 64
C = 256
HALF = 128
OWN = 8
NT = (((1,), (1,)), ((), ()))


def dot(x, y):
    return jnp.dot(x, y, preferred_element_type=F32)


def dot_nt(x, y):
    return lax.dot_general(x, y, NT, preferred_element_type=F32)


def shifted(x, by):
    n = x.shape[0]
    if by > 0:
        return jnp.concatenate([x[by:], jnp.zeros((by, x.shape[1]), x.dtype)], axis=0)
    return jnp.concatenate([jnp.zeros((-by, x.shape[1]), x.dtype), x[: n + by]], axis=0)


def put(ref, row, x, r, sign):
    ref[row, :, 0:C] = shifted(x, -sign * r)
    ref[row, :, C : 2 * C] = x
    ref[row, :, 2 * C : 3 * C] = shifted(x, sign * r)


def gate(h):
    p = 1.0 + jnp.tanh(h)
    return p, h * p


def slope2(p, silu):
    return p + silu * (2.0 - p)


def spans(rows, n):
    return [(t, min(n, rows - t)) for t in range(0, rows, n)]


def side_by_side(w, tap):
    return jnp.concatenate([w[tap + k] for k in range(9)], axis=1)


def body(
    info, msg, w_own, w_z, w_s, out,
    w, lcan, rcan, ccan, lwin, rwin, u_all, v_all, e0, e63,
    pp1, pp2, pd2, pd1, ds0, ds1, g2, p3, d0, g1h, g1l, rcv, lcv, ccv, sem,
):
    q, first, core, chan, total = info[0], info[1], info[2], info[3], info[4]
    mine = pl.ds(pl.multiple_of(chan * HALF, HALF), HALF)
    theirs = pl.ds(pl.multiple_of((1 - chan) * HALF, HALF), HALF)
    near = pl.ds(pl.multiple_of(core * HALF, HALF), HALF)
    far = pl.ds(pl.multiple_of((1 - core) * HALF, HALF), HALF)
    copies = []
    for k in range(3):
        taps = pl.ds(9 * k, 9)
        copies.append([
            pltpu.make_async_copy(w_own.at[taps], w.at[taps, :, mine], sem.at[k, 0]),
            pltpu.make_async_copy(w_z.at[taps], w.at[taps, near, theirs], sem.at[k, 1]),
            pltpu.make_async_copy(w_s.at[taps], w.at[taps, far, theirs], sem.at[k, 2]),
        ])
        for c in copies[k]:
            c.start()

    def valid(row):
        i = first + row
        return jnp.where((i >= 0) & (i < total), 1.0, 0.0)

    lcan[96:176] = jnp.zeros((80, C), F32)
    rcan[160:176] = jnp.zeros((16, C), F32)
    ccan[96:192] = jnp.zeros((96, HALF), F32)
    def place(ref, to, lanes, x):
        ref[to : to + 16, lanes] = x.astype(F32)

    for j in range(4):
        for g in range(2):
            e = 2 * j + g
            lanes = slice(HALF * g, HALF * g + HALF)
            place(lcan, 16 + 16 * j, lanes, msg[e, 0:16])
            place(rcan, 16 + 16 * j, lanes, msg[e, 16:32])
            place(rcan, 80 + 16 * j, lanes, msg[e, 48:64])
            if j == 0:
                place(lcan, 80, lanes, msg[e, 64:80])
            if j == 1:
                place(lcan, 0, lanes, msg[e, 64:80])
                place(rcan, 0, lanes, msg[e, 80:96])
            if j == 3:
                place(rcan, 144, lanes, msg[e, 80:96])
    for to, j, at in ((0, 1, 96), (16, 0, 32), (32, 1, 32), (48, 2, 32), (64, 3, 32), (80, 0, 96)):
        ccan[to : to + 16] = msg[2 * j, at : at + 16].astype(F32) + msg[2 * j + 1, at : at + 16].astype(F32)
    halves = []
    lane = lax.broadcasted_iota(jnp.int32, (1, HALF), 1)
    for g in range(2):
        m = msg[g, 32:48].astype(F32)
        even, odd = m[0:1] + m[2:3] + m[4:5], m[1:2] + m[3:4] + m[5:6]
        halves.append(jnp.where(lane < BAND, pltpu.roll(even, BAND, 1), odd))
    readout = jnp.concatenate(halves, axis=1)
    rest, parts = readout, []
    for _ in range(3):
        parts.append(rest.astype(BF).astype(F32))
        rest = rest - parts[-1]
    read_b = jnp.concatenate(parts + [jnp.zeros((13, C), F32)], axis=0).astype(BF)
    start = pl.multiple_of(q * OWN, OWN)
    lwin[...] = lcan[pl.ds(start, 48)]
    rwin[...] = rcan[pl.ds(start, 112)]
    cot_t = jnp.transpose(ccan[pl.ds(pl.multiple_of(start + 8, OWN), 128)])

    for c in copies[0]:
        c.wait()
    ul, va, vb = [None] * 3, [None] * 3, [None] * 3
    for b in range(3):
        for a in range(3):
            lhs = jnp.concatenate([lwin[2 + a : 42 + a], rwin[1 + a + b : 105 + a + b]], axis=0)
            y = dot(lhs.astype(BF), w[3 * a + b])
            ul[b] = y[:40] if a == 0 else ul[b] + y[:40]
            if a == 0:
                va[b] = y[40:]
            else:
                vb[b] = y[40:] if a == 1 else vb[b] + y[40:]
    u_all[...] = ul[0] + ul[1] + ul[2]
    for var in range(2):
        v = [vb[b] + va[b] if var == 0 else vb[b] for b in range(3)]
        v_all[var] = v[0] + v[1] + v[2]
        e0[var] = ul[1] + ul[2] + (v[1] + v[2])[:40]
        e63[var] = ul[0] + ul[1] + (v[0] + v[1])[63:103]
    tile = lax.broadcasted_iota(jnp.int32, (8, C), 0)

    def row_0(t):
        row = t - 13
        var = jnp.where(first + row == 0, 1, 0)
        pair = (lwin[t + 3 : t + 4] + rwin[t + 3 : t + 67]).astype(BF).astype(F32)
        pre = u_all[t : t + 1] + v_all[var, t : t + BAND]
        pre = jnp.concatenate(
            [
                jnp.where(tile == 0, e0[var, t : t + 1], pre[:8]),
                pre[8 : BAND - 8],
                jnp.where(tile == 7, e63[var, t : t + 1], pre[BAND - 8 :]),
            ],
            axis=0,
        )
        p, sil = gate(0.5 * pre)
        if 12 <= t < 22:
            ds0[t - 12] = slope2(p, sil).astype(BF)
        put(pp1, t, ((pair + sil) * valid(row)).astype(BF), 2, 1)

    for c in copies[1]:
        c.wait()
    done = 0
    for t0, n in spans(30, 3):
        while done < t0 + n + 4:
            row_0(done)
            done += 1
        x = [pp1[t0 + 2 * a : t0 + 2 * a + n].reshape(n * BAND, 3 * C) for a in range(3)]
        acc = dot(jnp.concatenate(x, axis=1), w[9:18].reshape(9 * C, C))
        for s in range(n):
            t = t0 + s
            p, sil = gate(0.5 * acc[s * BAND : (s + 1) * BAND])
            if 8 <= t < 22:
                ds1[t - 8] = slope2(p, sil).astype(BF)
            pair = pp1[t + 2, :, C : 2 * C].astype(F32)
            put(pp2, t, ((pair + sil) * valid(t - 11)).astype(BF), 4, 1)

    for c in copies[2]:
        c.wait()

    half = 0.5 * readout

    def top(row, scale):
        return cot_t[:BAND, row + 8 : row + 9] * scale

    for t0, n in spans(22, 4):
        x = [pp2[t0 + 4 * a : t0 + 4 * a + n].reshape(n * BAND, 3 * C) for a in range(3)]
        acc = dot(jnp.concatenate(x, axis=1), w[18:27].reshape(9 * C, C))
        for s in range(n):
            t = t0 + s
            p, sil = gate(0.5 * acc[s * BAND : (s + 1) * BAND])
            if 7 <= t < 15:
                p3[t - 7] = (pp2[t + 4, :, C : 2 * C].astype(F32) + sil).astype(BF)
            put(pd2, t, (top(t - 7, half) * slope2(p, sil)).astype(BF), 4, -1)
    ccv[...] = jnp.zeros((64, HALF), F32)
    rows = [jnp.sum(dot_nt(read_b, p3[s]), axis=0, keepdims=True) for s in range(OWN)]
    contact = jnp.concatenate(rows, axis=0)
    hi = contact.astype(BF).astype(F32)
    ccv[pl.ds(start, OWN)] = jnp.concatenate([hi, contact - hi], axis=1)

    for t0, n in spans(14, 5):
        x = [pd2[t0 + 8 - 4 * a : t0 + 8 - 4 * a + n].reshape(n * BAND, 3 * C) for a in range(3)]
        acc = dot_nt(jnp.concatenate(x, axis=1), side_by_side(w, 18))
        for s in range(n):
            t = t0 + s
            grad = top(t - 3, readout) + acc[s * BAND : (s + 1) * BAND]
            if 2 <= t < 12:
                g2[t - 2] = grad
            put(pd1, t, (grad * ds1[t].astype(F32) * (0.5 * valid(t - 3))).astype(BF), 2, -1)

    for t0, n in spans(10, 5):
        x = [pd1[t0 + 4 - 2 * a : t0 + 4 - 2 * a + n].reshape(n * BAND, 3 * C) for a in range(3)]
        acc = dot_nt(jnp.concatenate(x, axis=1), side_by_side(w, 9))
        for s in range(n):
            t = t0 + s
            grad = g2[t] + acc[s * BAND : (s + 1) * BAND]
            if 1 <= t < 9:
                hi = grad.astype(BF)
                g1h[t - 1] = hi
                g1l[t - 1] = (grad - hi.astype(F32)).astype(BF)
            d0[t] = (grad * ds0[t].astype(F32) * (0.5 * valid(t - 1))).astype(BF)

    def iotas(shape):
        at = lax.broadcasted_iota(jnp.int32, shape, 1)
        return lax.broadcasted_iota(jnp.int32, shape, 0), at >> 6, at & 63

    def ones(hit):
        return jnp.where(hit, 1.0, 0.0).astype(BF)

    to, i, d = iotas((80, 10 * BAND))
    key = to - i - d
    along = {s: ones(key == s) for s in range(-3, 2)}
    to, i, d = iotas((16, 10 * BAND))
    key = jnp.where(to < OWN, to - i, 99)
    across = [ones(key == a - 2) for a in range(3)]
    unused, i, d = iotas((1, 10 * BAND))
    in_d = [ones((d >= 1 - b) & (d < BAND + 1 - b)) for b in range(3)]
    in_i = [ones((i >= 2 - a) & (i < OWN + 2 - a)) for a in range(3)]
    picks = []
    for a in range(3):
        for b in range(3):
            picks.append(along[a + b - 3] * (in_i[a] * in_d[b]))
            picks.append(across[a] * in_d[b])
    z = dot(jnp.concatenate(picks, axis=0), d0[...].reshape(10 * BAND, C)).astype(BF)
    z = jnp.concatenate([z[96 * k : 96 * k + 96] for k in range(9)], axis=1)
    own = jnp.concatenate([along[-1][:, BAND : 9 * BAND], across[1][:, BAND : 9 * BAND]], axis=0)
    top96 = dot(own, g1h[...].reshape(OWN * BAND, C)) + dot(own, g1l[...].reshape(OWN * BAND, C))
    top96 = top96 + dot_nt(z, side_by_side(w, 0))
    rcv[...] = jnp.zeros((128, C), F32)
    lcv[...] = jnp.zeros((64, C), F32)
    rcv[pl.ds(start, 72)] = top96[:72]
    lcv[pl.ds(start, OWN)] = top96[80:88]
    for j in range(4):
        for g in range(2):
            lanes = slice(HALF * g, HALF * g + HALF)
            out[2 * j + g, 0:16] = rcv[16 * j : 16 * j + 16, lanes].astype(BF)
            out[2 * j + g, 16:32] = rcv[64 + 16 * j : 80 + 16 * j, lanes].astype(BF)
            out[2 * j + g, 32:48] = lcv[16 * j : 16 * j + 16, lanes].astype(BF)
            out[2 * j + g, 48:64] = ccv[16 * j : 16 * j + 16].astype(BF)


def local_part(info, msg, w_own, w_z, w_s):
    vm = pltpu.VMEM
    scratch = [
        vm((27, C, C), BF),
        vm((176, C), F32),
        vm((176, C), F32),
        vm((192, HALF), F32),
        vm((48, C), F32),
        vm((112, C), F32),
        vm((40, C), F32),
        vm((2, 104, C), F32),
        vm((2, 40, C), F32),
        vm((2, 40, C), F32),
        vm((34, BAND, 3 * C), BF),
        vm((30, BAND, 3 * C), BF),
        vm((22, BAND, 3 * C), BF),
        vm((14, BAND, 3 * C), BF),
        vm((10, BAND, C), BF),
        vm((14, BAND, C), BF),
        vm((10, BAND, C), F32),
        vm((8, BAND, C), BF),
        vm((10, BAND, C), BF),
        vm((8, BAND, C), BF),
        vm((8, BAND, C), BF),
        vm((128, C), F32),
        vm((64, C), F32),
        vm((64, HALF), F32),
        pltpu.SemaphoreType.DMA((3, 3)),
    ]
    return pl.pallas_call(
        body,
        out_shape=jax.ShapeDtypeStruct((8, 64, HALF), BF),
        in_specs=[
            pl.BlockSpec(memory_space=pltpu.SMEM),
            pl.BlockSpec(memory_space=vm),
            pl.BlockSpec(memory_space=pl.ANY),
            pl.BlockSpec(memory_space=pl.ANY),
            pl.BlockSpec(memory_space=pl.ANY),
        ],
        out_specs=pl.BlockSpec(memory_space=vm),
        scratch_shapes=scratch,
        compiler_params=pltpu.CompilerParams(vmem_limit_bytes=48 * 2**20),
        cost_estimate=pl.CostEstimate(
            flops=6 * 10**9, bytes_accessed=5 * 10**6, transcendentals=2 * 10**6
        ),
        name="decoder",
    )(info, msg, w_own, w_z, w_s)


def z_pairs(chroms):
    pairs = []
    per_z = chroms // 4
    for ch in range(chroms):
        hi, rest = ch // per_z, ch % per_z
        for g in range(2):
            step = (1 if g == 0 else -1) * (1 if ch % 2 == 0 else -1)
            z = (2 * hi + g + step) % 8
            pairs.append((((z // 2) * per_z + rest) * 2 + z % 2, 2 * ch + g))
    return pairs


def copy_half(core, w_own, out, sem):
    moves = [
        pltpu.make_async_copy(
            w_own.at[pl.ds(3 * k, 3), pl.ds(pl.multiple_of(core[0] * HALF, HALF), HALF)],
            out.at[pl.ds(3 * k, 3)],
            sem.at[k],
        )
        for k in range(9)
    ]
    for move in moves:
        move.start()
    for move in moves:
        move.wait()


def own_part(core, w_own):
    return pl.pallas_call(
        copy_half,
        out_shape=pltpu.VMEM((27, HALF, HALF), BF),
        in_specs=[pl.BlockSpec(memory_space=pltpu.SMEM), pl.BlockSpec(memory_space=pl.ANY)],
        out_specs=pl.BlockSpec(memory_space=pltpu.VMEM),
        scratch_shapes=[pltpu.SemaphoreType.DMA((9,))],
        cost_estimate=pl.CostEstimate(flops=0, bytes_accessed=2 * 10**6, transcendentals=0),
        name="own_part",
    )(core, w_own)


def parts_of(x, count):
    parts = []
    for _ in range(count):
        hi = lax.reduce_precision(x, 8, 7)
        parts.append(hi.astype(BF))
        x = x - hi
    return parts


def local(left, right, weight, readout, cotangent):
    rows = left.shape[0]
    chroms = lax.axis_size(CHROM)
    slab = lax.axis_index(CHROM)
    core = lax.axis_index("core")
    chan = lax.axis_index("chan")
    own_w = weight.reshape(27, C, HALF)
    piece = own_part(core[None].astype(jnp.int32), own_w)
    piece, readout, cotangent = lax.optimization_barrier((piece, readout, cotangent))

    hi, lo = parts_of(cotangent, 2)
    read = jnp.pad(jnp.stack(parts_of(readout, 3)).reshape(6, BAND), ((0, rows - 6), (0, 0)))
    cot = jnp.concatenate([jnp.where(chan == 0, hi, lo), read], axis=1)
    mine = jnp.concatenate([left, right, cot], axis=0)
    piece, mine = lax.optimization_barrier((piece, mine))
    w_z = lax.ppermute(piece, "chan", [(0, 1), (1, 0)])
    slabs = 4
    groups = chroms // slabs
    next_group = [
        (slabs * (g + 1) + j, slabs * g + j) for g in range(groups - 1) for j in range(slabs)
    ]
    ends = [(slabs * g + 3, slabs * (g + 1) + 1) for g in range(groups - 1)]
    ends += [(slabs * (g + 2), slabs * g + 3) for g in range(groups - 2)]
    after = lax.ppermute(mine, CHROM, next_group)
    edge = lax.ppermute(mine, CHROM, ends)
    extra = jnp.where(slab % slabs == 0, after, edge)
    block = jnp.concatenate([mine, after[rows : 2 * rows], extra], axis=0)
    msg = lax.all_to_all(
        jnp.broadcast_to(block[None], (8,) + block.shape), GROUP, 0, 0, tiled=False
    )
    msg, w_z = lax.optimization_barrier((msg, w_z))
    w_s = lax.ppermute(w_z, "core", [(0, 1), (1, 0)])
    q = lax.axis_index(GROUP)
    info = jnp.stack(
        [q, rows * slab + OWN * chan, core, chan, rows * chroms]
    ).astype(jnp.int32)
    sent = local_part(info, msg, own_w, w_z, w_s)
    got = jnp.sum(lax.all_to_all(sent, GROUP, 0, 0, tiled=False).astype(F32), axis=0)
    moved = lax.ppermute(got[16:32], CHROM, [(b, a) for a, b in next_group])
    return got[48:64, :BAND] + got[48:64, BAND:], got[32:48], got[0:16] + moved


def solution(mesh):
    chroms = mesh.shape["chrom"]
    small = Mesh(
        mesh.devices.reshape(chroms // 16, 4, 2, 2, 2), ("h", "yh", "yl", "core", "chan")
    )
    return jax.shard_map(
        local,
        mesh=small,
        in_specs=(
            P(CHROM, "chan"),
            P(CHROM, "chan"),
            P(None, None, None, None, "chan"),
            P("chan"),
            P(CHROM, None),
        ),
        out_specs=(P(CHROM, None), P(CHROM, "chan"), P(CHROM, "chan")),
        check_vma=False,
    )
```

```python
import jax
import jax.numpy as jnp
from jax import lax
from jax.experimental import pallas as pl
from jax.experimental.pallas import tpu as pltpu
from jax.sharding import Mesh, PartitionSpec as P

BF = jnp.bfloat16
F32 = jnp.float32
CHROM = ("h", "yh", "yl", "core")
GROUP = ("yl", "core", "chan")
ALL = CHROM + ("chan",)
BAND = 64
C = 256
HALF = 128
OWN = 8
NT = (((1,), (1,)), ((), ()))


def dot(x, y):
    return jnp.dot(x, y, preferred_element_type=F32)


def dot_nt(x, y):
    return lax.dot_general(x, y, NT, preferred_element_type=F32)


def shifted(x, by):
    n = x.shape[0]
    if by > 0:
        return jnp.concatenate([x[by:], jnp.zeros((by, x.shape[1]), x.dtype)], axis=0)
    return jnp.concatenate([jnp.zeros((-by, x.shape[1]), x.dtype), x[: n + by]], axis=0)


def put(ref, row, x, r, sign):
    ref[row, :, 0:C] = shifted(x, -sign * r)
    ref[row, :, C : 2 * C] = x
    ref[row, :, 2 * C : 3 * C] = shifted(x, sign * r)


def gate(h):
    p = 1.0 + jnp.tanh(h)
    return p, h * p


def slope2(p, silu):
    return p + silu * (2.0 - p)


def spans(rows, n):
    return [(t, min(n, rows - t)) for t in range(0, rows, n)]


def side_by_side(w, tap):
    return jnp.concatenate([w[tap + k] for k in range(9)], axis=1)


def body(
    info, msg, w_own, w_z, w_s, out,
    w, lcan, rcan, ccan, lwin, rwin, u_all, v_all, e0, e63,
    pp1, pp2, pd2, pd1, ds0, ds1, g2, p3, d0, g1h, g1l, rcv, lcv, ccv, sem,
):
    q, first, core, chan, total = info[0], info[1], info[2], info[3], info[4]
    mine = pl.ds(pl.multiple_of(chan * HALF, HALF), HALF)
    theirs = pl.ds(pl.multiple_of((1 - chan) * HALF, HALF), HALF)
    near = pl.ds(pl.multiple_of(core * HALF, HALF), HALF)
    far = pl.ds(pl.multiple_of((1 - core) * HALF, HALF), HALF)
    copies = []
    for k in range(3):
        taps = pl.ds(9 * k, 9)
        copies.append([
            pltpu.make_async_copy(w_own.at[taps], w.at[taps, :, mine], sem.at[k, 0]),
            pltpu.make_async_copy(w_z.at[taps], w.at[taps, near, theirs], sem.at[k, 1]),
            pltpu.make_async_copy(w_s.at[taps], w.at[taps, far, theirs], sem.at[k, 2]),
        ])
        for c in copies[k]:
            c.start()

    def valid(row):
        i = first + row
        return jnp.where((i >= 0) & (i < total), 1.0, 0.0)

    lcan[96:176] = jnp.zeros((80, C), F32)
    rcan[160:176] = jnp.zeros((16, C), F32)
    ccan[96:192] = jnp.zeros((96, HALF), F32)
    def place(ref, to, lanes, x):
        ref[to : to + 16, lanes] = x.astype(F32)

    for j in range(4):
        for g in range(2):
            e = 2 * j + g
            lanes = slice(HALF * g, HALF * g + HALF)
            place(lcan, 16 + 16 * j, lanes, msg[e, 0:16])
            place(rcan, 16 + 16 * j, lanes, msg[e, 16:32])
            place(rcan, 80 + 16 * j, lanes, msg[e, 48:64])
            if j == 0:
                place(lcan, 80, lanes, msg[e, 64:80])
            if j == 1:
                place(lcan, 0, lanes, msg[e, 64:80])
                place(rcan, 0, lanes, msg[e, 80:96])
            if j == 3:
                place(rcan, 144, lanes, msg[e, 80:96])
    for to, j, at in ((0, 1, 96), (16, 0, 32), (32, 1, 32), (48, 2, 32), (64, 3, 32), (80, 0, 96)):
        ccan[to : to + 16] = msg[2 * j, at : at + 16].astype(F32) + msg[2 * j + 1, at : at + 16].astype(F32)
    halves = []
    lane = lax.broadcasted_iota(jnp.int32, (1, HALF), 1)
    for g in range(2):
        m = msg[g, 32:48].astype(F32)
        even, odd = m[0:1] + m[2:3] + m[4:5], m[1:2] + m[3:4] + m[5:6]
        halves.append(jnp.where(lane < BAND, pltpu.roll(even, BAND, 1), odd))
    readout = jnp.concatenate(halves, axis=1)
    rest, parts = readout, []
    for _ in range(3):
        parts.append(rest.astype(BF).astype(F32))
        rest = rest - parts[-1]
    read_b = jnp.concatenate(parts + [jnp.zeros((13, C), F32)], axis=0).astype(BF)
    start = pl.multiple_of(q * OWN, OWN)
    lwin[...] = lcan[pl.ds(start, 48)]
    rwin[...] = rcan[pl.ds(start, 112)]
    cot_t = jnp.transpose(ccan[pl.ds(pl.multiple_of(start + 8, OWN), 128)])

    for c in copies[0]:
        c.wait()
    ul, va, vb = [None] * 3, [None] * 3, [None] * 3
    for b in range(3):
        for a in range(3):
            lhs = jnp.concatenate([lwin[2 + a : 42 + a], rwin[1 + a + b : 105 + a + b]], axis=0)
            y = dot(lhs.astype(BF), w[3 * a + b])
            ul[b] = y[:40] if a == 0 else ul[b] + y[:40]
            if a == 0:
                va[b] = y[40:]
            else:
                vb[b] = y[40:] if a == 1 else vb[b] + y[40:]
    u_all[...] = 0.5 * (ul[0] + ul[1] + ul[2])
    for var in range(2):
        v = [vb[b] + va[b] if var == 0 else vb[b] for b in range(3)]
        v_all[var] = 0.5 * (v[0] + v[1] + v[2])
        e0[var] = 0.5 * (ul[1] + ul[2] + (v[1] + v[2])[:40])
        e63[var] = 0.5 * (ul[0] + ul[1] + (v[0] + v[1])[63:103])
    tile = lax.broadcasted_iota(jnp.int32, (8, C), 0)

    def row_0(t):
        row = t - 13
        var = jnp.where(first + row == 0, 1, 0)
        pair = (lwin[t + 3 : t + 4] + rwin[t + 3 : t + 67]).astype(BF).astype(F32)
        pre = u_all[t : t + 1] + v_all[var, t : t + BAND]
        pre = jnp.concatenate(
            [
                jnp.where(tile == 0, e0[var, t : t + 1], pre[:8]),
                pre[8 : BAND - 8],
                jnp.where(tile == 7, e63[var, t : t + 1], pre[BAND - 8 :]),
            ],
            axis=0,
        )
        p, sil = gate(pre)
        if 12 <= t < 22:
            ds0[t - 12] = slope2(p, sil).astype(BF)
        put(pp1, t, (pair + sil).astype(BF) * valid(row).astype(BF), 2, 1)

    for c in copies[1]:
        c.wait()
    done = 0
    for t0, n in spans(30, 3):
        while done < t0 + n + 4:
            row_0(done)
            done += 1
        x = [pp1[t0 + 2 * a : t0 + 2 * a + n].reshape(n * BAND, 3 * C) for a in range(3)]
        acc = dot(jnp.concatenate(x, axis=1), w[9:18].reshape(9 * C, C))
        for s in range(n):
            t = t0 + s
            p, sil = gate(0.5 * acc[s * BAND : (s + 1) * BAND])
            if 8 <= t < 22:
                ds1[t - 8] = slope2(p, sil).astype(BF)
            pair = pp1[t + 2, :, C : 2 * C].astype(F32)
            put(pp2, t, (pair + sil).astype(BF) * valid(t - 11).astype(BF), 4, 1)

    for c in copies[2]:
        c.wait()

    half = 0.5 * readout

    def top(row, scale):
        return cot_t[:BAND, row + 8 : row + 9] * scale

    for t0, n in spans(22, 4):
        x = [pp2[t0 + 4 * a : t0 + 4 * a + n].reshape(n * BAND, 3 * C) for a in range(3)]
        acc = dot(jnp.concatenate(x, axis=1), w[18:27].reshape(9 * C, C))
        for s in range(n):
            t = t0 + s
            p, sil = gate(0.5 * acc[s * BAND : (s + 1) * BAND])
            if 7 <= t < 15:
                p3[t - 7] = (pp2[t + 4, :, C : 2 * C].astype(F32) + sil).astype(BF)
            put(pd2, t, (top(t - 7, half) * slope2(p, sil)).astype(BF), 4, -1)
    ccv[...] = jnp.zeros((64, HALF), F32)
    rows = [jnp.sum(dot_nt(read_b, p3[s]), axis=0, keepdims=True) for s in range(OWN)]
    contact = jnp.concatenate(rows, axis=0)
    hi = contact.astype(BF).astype(F32)
    ccv[pl.ds(start, OWN)] = jnp.concatenate([hi, contact - hi], axis=1)

    for t0, n in spans(14, 5):
        x = [pd2[t0 + 8 - 4 * a : t0 + 8 - 4 * a + n].reshape(n * BAND, 3 * C) for a in range(3)]
        acc = dot_nt(jnp.concatenate(x, axis=1), side_by_side(w, 18))
        for s in range(n):
            t = t0 + s
            grad = top(t - 3, readout) + acc[s * BAND : (s + 1) * BAND]
            if 2 <= t < 12:
                g2[t - 2] = grad
            put(pd1, t, (grad * ds1[t].astype(F32) * (0.5 * valid(t - 3))).astype(BF), 2, -1)

    for t0, n in spans(10, 5):
        x = [pd1[t0 + 4 - 2 * a : t0 + 4 - 2 * a + n].reshape(n * BAND, 3 * C) for a in range(3)]
        acc = dot_nt(jnp.concatenate(x, axis=1), side_by_side(w, 9))
        for s in range(n):
            t = t0 + s
            grad = g2[t] + acc[s * BAND : (s + 1) * BAND]
            if 1 <= t < 9:
                hi = grad.astype(BF)
                g1h[t - 1] = hi
                g1l[t - 1] = (grad - hi.astype(F32)).astype(BF)
            d0[t] = (grad * ds0[t].astype(F32) * (0.5 * valid(t - 1))).astype(BF)

    def iotas(shape):
        at = lax.broadcasted_iota(jnp.int32, shape, 1)
        return lax.broadcasted_iota(jnp.int32, shape, 0), at >> 6, at & 63

    def ones(hit):
        return jnp.where(hit, 1.0, 0.0).astype(BF)

    to, i, d = iotas((80, 10 * BAND))
    key = to - i - d
    along = {s: ones(key == s) for s in range(-3, 2)}
    to, i, d = iotas((16, 10 * BAND))
    key = jnp.where(to < OWN, to - i, 99)
    across = [ones(key == a - 2) for a in range(3)]
    unused, i, d = iotas((1, 10 * BAND))
    in_d = [ones((d >= 1 - b) & (d < BAND + 1 - b)) for b in range(3)]
    in_i = [ones((i >= 2 - a) & (i < OWN + 2 - a)) for a in range(3)]
    picks = []
    for a in range(3):
        for b in range(3):
            picks.append(along[a + b - 3] * (in_i[a] * in_d[b]))
            picks.append(across[a] * in_d[b])
    z = dot(jnp.concatenate(picks, axis=0), d0[...].reshape(10 * BAND, C)).astype(BF)
    z = jnp.concatenate([z[96 * k : 96 * k + 96] for k in range(9)], axis=1)
    own = jnp.concatenate([along[-1][:, BAND : 9 * BAND], across[1][:, BAND : 9 * BAND]], axis=0)
    top96 = dot(own, g1h[...].reshape(OWN * BAND, C)) + dot(own, g1l[...].reshape(OWN * BAND, C))
    top96 = top96 + dot_nt(z, side_by_side(w, 0))
    rcv[...] = jnp.zeros((128, C), F32)
    lcv[...] = jnp.zeros((64, C), F32)
    rcv[pl.ds(start, 72)] = top96[:72]
    lcv[pl.ds(start, OWN)] = top96[80:88]
    for j in range(4):
        for g in range(2):
            lanes = slice(HALF * g, HALF * g + HALF)
            out[2 * j + g, 0:16] = rcv[16 * j : 16 * j + 16, lanes].astype(BF)
            out[2 * j + g, 16:32] = rcv[64 + 16 * j : 80 + 16 * j, lanes].astype(BF)
            out[2 * j + g, 32:48] = lcv[16 * j : 16 * j + 16, lanes].astype(BF)
            out[2 * j + g, 48:64] = ccv[16 * j : 16 * j + 16].astype(BF)


def local_part(info, msg, w_own, w_z, w_s):
    vm = pltpu.VMEM
    scratch = [
        vm((27, C, C), BF),
        vm((176, C), F32),
        vm((176, C), F32),
        vm((192, HALF), F32),
        vm((48, C), F32),
        vm((112, C), F32),
        vm((40, C), F32),
        vm((2, 104, C), F32),
        vm((2, 40, C), F32),
        vm((2, 40, C), F32),
        vm((34, BAND, 3 * C), BF),
        vm((30, BAND, 3 * C), BF),
        vm((22, BAND, 3 * C), BF),
        vm((14, BAND, 3 * C), BF),
        vm((10, BAND, C), BF),
        vm((14, BAND, C), BF),
        vm((10, BAND, C), F32),
        vm((8, BAND, C), BF),
        vm((10, BAND, C), BF),
        vm((8, BAND, C), BF),
        vm((8, BAND, C), BF),
        vm((128, C), F32),
        vm((64, C), F32),
        vm((64, HALF), F32),
        pltpu.SemaphoreType.DMA((3, 3)),
    ]
    return pl.pallas_call(
        body,
        out_shape=jax.ShapeDtypeStruct((8, 64, HALF), BF),
        in_specs=[
            pl.BlockSpec(memory_space=pltpu.SMEM),
            pl.BlockSpec(memory_space=vm),
            pl.BlockSpec(memory_space=pl.ANY),
            pl.BlockSpec(memory_space=pl.ANY),
            pl.BlockSpec(memory_space=pl.ANY),
        ],
        out_specs=pl.BlockSpec(memory_space=vm),
        scratch_shapes=scratch,
        compiler_params=pltpu.CompilerParams(vmem_limit_bytes=48 * 2**20),
        cost_estimate=pl.CostEstimate(
            flops=6 * 10**9, bytes_accessed=5 * 10**6, transcendentals=2 * 10**6
        ),
        name="decoder",
    )(info, msg, w_own, w_z, w_s)


def z_pairs(chroms):
    pairs = []
    per_z = chroms // 4
    for ch in range(chroms):
        hi, rest = ch // per_z, ch % per_z
        for g in range(2):
            step = (1 if g == 0 else -1) * (1 if ch % 2 == 0 else -1)
            z = (2 * hi + g + step) % 8
            pairs.append((((z // 2) * per_z + rest) * 2 + z % 2, 2 * ch + g))
    return pairs


def copy_half(core, w_own, out, sem):
    moves = [
        pltpu.make_async_copy(
            w_own.at[pl.ds(3 * k, 3), pl.ds(pl.multiple_of(core[0] * HALF, HALF), HALF)],
            out.at[pl.ds(3 * k, 3)],
            sem.at[k],
        )
        for k in range(9)
    ]
    for move in moves:
        move.start()
    for move in moves:
        move.wait()


def own_part(core, w_own):
    return pl.pallas_call(
        copy_half,
        out_shape=pltpu.VMEM((27, HALF, HALF), BF),
        in_specs=[pl.BlockSpec(memory_space=pltpu.SMEM), pl.BlockSpec(memory_space=pl.ANY)],
        out_specs=pl.BlockSpec(memory_space=pltpu.VMEM),
        scratch_shapes=[pltpu.SemaphoreType.DMA((9,))],
        cost_estimate=pl.CostEstimate(flops=0, bytes_accessed=2 * 10**6, transcendentals=0),
        name="own_part",
    )(core, w_own)


def parts_of(x, count):
    parts = []
    for _ in range(count):
        hi = lax.reduce_precision(x, 8, 7)
        parts.append(hi.astype(BF))
        x = x - hi
    return parts


def local(left, right, weight, readout, cotangent):
    rows = left.shape[0]
    chroms = lax.axis_size(CHROM)
    slab = lax.axis_index(CHROM)
    core = lax.axis_index("core")
    chan = lax.axis_index("chan")
    own_w = weight.reshape(27, C, HALF)
    piece = own_part(core[None].astype(jnp.int32), own_w)
    piece, readout, cotangent = lax.optimization_barrier((piece, readout, cotangent))

    hi, lo = parts_of(cotangent, 2)
    read = jnp.pad(jnp.stack(parts_of(readout, 3)).reshape(6, BAND), ((0, rows - 6), (0, 0)))
    cot = jnp.concatenate([jnp.where(chan == 0, hi, lo), read], axis=1)
    mine = jnp.concatenate([left, right, cot], axis=0)
    piece, mine = lax.optimization_barrier((piece, mine))
    w_z = lax.ppermute(piece, "chan", [(0, 1), (1, 0)])
    slabs = 4
    groups = chroms // slabs
    next_group = [
        (slabs * (g + 1) + j, slabs * g + j) for g in range(groups - 1) for j in range(slabs)
    ]
    ends = [(slabs * g + 3, slabs * (g + 1) + 1) for g in range(groups - 1)]
    ends += [(slabs * (g + 2), slabs * g + 3) for g in range(groups - 2)]
    after = lax.ppermute(mine, CHROM, next_group)
    edge = lax.ppermute(mine, CHROM, ends)
    extra = jnp.where(slab % slabs == 0, after, edge)
    block = jnp.concatenate([mine, after[rows : 2 * rows], extra], axis=0)
    msg = lax.all_to_all(
        jnp.broadcast_to(block[None], (8,) + block.shape), GROUP, 0, 0, tiled=False
    )
    msg, w_z = lax.optimization_barrier((msg, w_z))
    w_s = lax.ppermute(w_z, "core", [(0, 1), (1, 0)])
    q = lax.axis_index(GROUP)
    info = jnp.stack(
        [q, rows * slab + OWN * chan, core, chan, rows * chroms]
    ).astype(jnp.int32)
    sent = local_part(info, msg, own_w, w_z, w_s)
    got = jnp.sum(lax.all_to_all(sent, GROUP, 0, 0, tiled=False).astype(F32), axis=0)
    moved = lax.ppermute(got[16:32], CHROM, [(b, a) for a, b in next_group])
    return got[48:64, :BAND] + got[48:64, BAND:], got[32:48], got[0:16] + moved


def solution(mesh):
    chroms = mesh.shape["chrom"]
    small = Mesh(
        mesh.devices.reshape(chroms // 16, 4, 2, 2, 2), ("h", "yh", "yl", "core", "chan")
    )
    return jax.shard_map(
        local,
        mesh=small,
        in_specs=(
            P(CHROM, "chan"),
            P(CHROM, "chan"),
            P(None, None, None, None, "chan"),
            P("chan"),
            P(CHROM, None),
        ),
        out_specs=(P(CHROM, None), P(CHROM, "chan"), P(CHROM, "chan")),
        check_vma=False,
    )
```

```python
import jax
import jax.numpy as jnp
from jax import lax
from jax.experimental import pallas as pl
from jax.experimental.pallas import tpu as pltpu
from jax.sharding import Mesh, PartitionSpec as P

BF = jnp.bfloat16
F32 = jnp.float32
CHROM = ("h", "yh", "yl", "core")
GROUP = ("chan", "yl", "core")
ALL = CHROM + ("chan",)
BAND = 64
C = 256
HALF = 128
OWN = 8
NT = (((1,), (1,)), ((), ()))


def dot(x, y):
    return jnp.dot(x, y, preferred_element_type=F32)


def dot_nt(x, y):
    return lax.dot_general(x, y, NT, preferred_element_type=F32)


def shifted(x, by):
    n = x.shape[0]
    if by > 0:
        return jnp.concatenate([x[by:], jnp.zeros((by, x.shape[1]), x.dtype)], axis=0)
    return jnp.concatenate([jnp.zeros((-by, x.shape[1]), x.dtype), x[: n + by]], axis=0)


def put(ref, row, x, r, sign):
    ref[row, :, 0:C] = shifted(x, -sign * r)
    ref[row, :, C : 2 * C] = x
    ref[row, :, 2 * C : 3 * C] = shifted(x, sign * r)


def gate(h):
    p = 1.0 + jnp.tanh(h)
    return p, h * p


def slope2(p, silu):
    return p + silu * (2.0 - p)


def spans(rows, n):
    return [(t, min(n, rows - t)) for t in range(0, rows, n)]


def side_by_side(w, tap):
    return jnp.concatenate([w[tap + k] for k in range(9)], axis=1)


def body(
    info, msg, w_own, w_z, w_s, out,
    w, lcan, rcan, ccan, lwin, rwin, u_all, v_all, e0, e63,
    pp1, pp2, pd2, pd1, ds0, ds1, g2, p3, d0, g1h, g1l, rcv, lcv, ccv, sem,
):
    q, first, core, chan, total = info[0], info[1], info[2], info[3], info[4]
    mine = pl.ds(pl.multiple_of(chan * HALF, HALF), HALF)
    theirs = pl.ds(pl.multiple_of((1 - chan) * HALF, HALF), HALF)
    near = pl.ds(pl.multiple_of(core * HALF, HALF), HALF)
    far = pl.ds(pl.multiple_of((1 - core) * HALF, HALF), HALF)
    copies = []
    for k in range(3):
        taps = pl.ds(9 * k, 9)
        copies.append([
            pltpu.make_async_copy(w_own.at[taps], w.at[taps, :, mine], sem.at[k, 0]),
            pltpu.make_async_copy(w_z.at[taps], w.at[taps, near, theirs], sem.at[k, 1]),
            pltpu.make_async_copy(w_s.at[taps], w.at[taps, far, theirs], sem.at[k, 2]),
        ])
        for c in copies[k]:
            c.start()

    def valid(row):
        i = first + row
        return jnp.where((i >= 0) & (i < total), 1.0, 0.0)

    lcan[96:176] = jnp.zeros((80, C), F32)
    rcan[160:176] = jnp.zeros((16, C), F32)
    ccan[96:192] = jnp.zeros((96, HALF), F32)
    def place(ref, to, lanes, x):
        ref[to : to + 16, lanes] = x.astype(F32)

    for j in range(4):
        for g in range(2):
            e = 4 * g + j
            lanes = slice(HALF * g, HALF * g + HALF)
            place(lcan, 16 + 16 * j, lanes, msg[e, 0:16])
            place(rcan, 16 + 16 * j, lanes, msg[e, 16:32])
            place(rcan, 80 + 16 * j, lanes, msg[e, 48:64])
            if j == 0:
                place(lcan, 80, lanes, msg[e, 64:80])
            if j == 1:
                place(lcan, 0, lanes, msg[e, 64:80])
                place(rcan, 0, lanes, msg[e, 80:96])
            if j == 3:
                place(rcan, 144, lanes, msg[e, 80:96])
    for to, j, at in ((0, 1, 96), (16, 0, 32), (32, 1, 32), (48, 2, 32), (64, 3, 32), (80, 0, 96)):
        ccan[to : to + 16] = msg[j, at : at + 16].astype(F32) + msg[4 + j, at : at + 16].astype(F32)
    halves = []
    lane = lax.broadcasted_iota(jnp.int32, (1, HALF), 1)
    for g in range(2):
        m = msg[4 * g, 32:48].astype(F32)
        even, odd = m[0:1] + m[2:3] + m[4:5], m[1:2] + m[3:4] + m[5:6]
        halves.append(jnp.where(lane < BAND, pltpu.roll(even, BAND, 1), odd))
    readout = jnp.concatenate(halves, axis=1)
    rest, parts = readout, []
    for _ in range(3):
        parts.append(rest.astype(BF).astype(F32))
        rest = rest - parts[-1]
    read_b = jnp.concatenate(parts + [jnp.zeros((13, C), F32)], axis=0).astype(BF)
    start = pl.multiple_of(q * OWN, OWN)
    lwin[...] = lcan[pl.ds(start, 48)]
    rwin[...] = rcan[pl.ds(start, 112)]
    cot_t = jnp.transpose(ccan[pl.ds(pl.multiple_of(start + 8, OWN), 128)])

    for c in copies[0]:
        c.wait()
    ul, va, vb = [None] * 3, [None] * 3, [None] * 3
    for b in range(3):
        for a in range(3):
            lhs = jnp.concatenate([lwin[2 + a : 42 + a], rwin[1 + a + b : 105 + a + b]], axis=0)
            y = dot(lhs.astype(BF), w[3 * a + b])
            ul[b] = y[:40] if a == 0 else ul[b] + y[:40]
            if a == 0:
                va[b] = y[40:]
            else:
                vb[b] = y[40:] if a == 1 else vb[b] + y[40:]
    u_all[...] = 0.5 * (ul[0] + ul[1] + ul[2])
    for var in range(2):
        v = [vb[b] + va[b] if var == 0 else vb[b] for b in range(3)]
        v_all[var] = 0.5 * (v[0] + v[1] + v[2])
        e0[var] = 0.5 * (ul[1] + ul[2] + (v[1] + v[2])[:40])
        e63[var] = 0.5 * (ul[0] + ul[1] + (v[0] + v[1])[63:103])
    tile = lax.broadcasted_iota(jnp.int32, (8, C), 0)

    def row_0(t):
        row = t - 13
        var = jnp.where(first + row == 0, 1, 0)
        pair = (lwin[t + 3 : t + 4] + rwin[t + 3 : t + 67]).astype(BF).astype(F32)
        pre = u_all[t : t + 1] + v_all[var, t : t + BAND]
        pre = jnp.concatenate(
            [
                jnp.where(tile == 0, e0[var, t : t + 1], pre[:8]),
                pre[8 : BAND - 8],
                jnp.where(tile == 7, e63[var, t : t + 1], pre[BAND - 8 :]),
            ],
            axis=0,
        )
        p, sil = gate(pre)
        if 12 <= t < 22:
            ds0[t - 12] = slope2(p, sil).astype(BF)
        put(pp1, t, (pair + sil).astype(BF) * valid(row).astype(BF), 2, 1)

    for c in copies[1]:
        c.wait()
    done = 0
    for t0, n in spans(30, 3):
        while done < t0 + n + 4:
            row_0(done)
            done += 1
        x = [pp1[t0 + 2 * a : t0 + 2 * a + n].reshape(n * BAND, 3 * C) for a in range(3)]
        acc = dot(jnp.concatenate(x, axis=1), w[9:18].reshape(9 * C, C))
        for s in range(n):
            t = t0 + s
            p, sil = gate(0.5 * acc[s * BAND : (s + 1) * BAND])
            if 8 <= t < 22:
                ds1[t - 8] = slope2(p, sil).astype(BF)
            pair = pp1[t + 2, :, C : 2 * C].astype(F32)
            put(pp2, t, (pair + sil).astype(BF) * valid(t - 11).astype(BF), 4, 1)

    for c in copies[2]:
        c.wait()

    half = 0.5 * readout

    def top(row, scale):
        return cot_t[:BAND, row + 8 : row + 9] * scale

    for t0, n in spans(22, 4):
        x = [pp2[t0 + 4 * a : t0 + 4 * a + n].reshape(n * BAND, 3 * C) for a in range(3)]
        acc = dot(jnp.concatenate(x, axis=1), w[18:27].reshape(9 * C, C))
        for s in range(n):
            t = t0 + s
            p, sil = gate(0.5 * acc[s * BAND : (s + 1) * BAND])
            if 7 <= t < 15:
                p3[t - 7] = (pp2[t + 4, :, C : 2 * C].astype(F32) + sil).astype(BF)
            put(pd2, t, (top(t - 7, half) * slope2(p, sil)).astype(BF), 4, -1)
    ccv[...] = jnp.zeros((64, HALF), F32)
    rows = [jnp.sum(dot_nt(read_b, p3[s]), axis=0, keepdims=True) for s in range(OWN)]
    contact = jnp.concatenate(rows, axis=0)
    hi = contact.astype(BF).astype(F32)
    ccv[pl.ds(start, OWN)] = jnp.concatenate([hi, contact - hi], axis=1)

    for t0, n in spans(14, 5):
        x = [pd2[t0 + 8 - 4 * a : t0 + 8 - 4 * a + n].reshape(n * BAND, 3 * C) for a in range(3)]
        acc = dot_nt(jnp.concatenate(x, axis=1), side_by_side(w, 18))
        for s in range(n):
            t = t0 + s
            grad = top(t - 3, readout) + acc[s * BAND : (s + 1) * BAND]
            if 2 <= t < 12:
                g2[t - 2] = grad
            put(pd1, t, (grad * ds1[t].astype(F32) * (0.5 * valid(t - 3))).astype(BF), 2, -1)

    for t0, n in spans(10, 5):
        x = [pd1[t0 + 4 - 2 * a : t0 + 4 - 2 * a + n].reshape(n * BAND, 3 * C) for a in range(3)]
        acc = dot_nt(jnp.concatenate(x, axis=1), side_by_side(w, 9))
        for s in range(n):
            t = t0 + s
            grad = g2[t] + acc[s * BAND : (s + 1) * BAND]
            if 1 <= t < 9:
                hi = grad.astype(BF)
                g1h[t - 1] = hi
                g1l[t - 1] = (grad - hi.astype(F32)).astype(BF)
            d0[t] = (grad * ds0[t].astype(F32) * (0.5 * valid(t - 1))).astype(BF)

    def iotas(shape):
        at = lax.broadcasted_iota(jnp.int32, shape, 1)
        return lax.broadcasted_iota(jnp.int32, shape, 0), at >> 6, at & 63

    def ones(hit):
        return jnp.where(hit, 1.0, 0.0).astype(BF)

    to, i, d = iotas((80, 10 * BAND))
    key = to - i - d
    along = {s: ones(key == s) for s in range(-3, 2)}
    to, i, d = iotas((16, 10 * BAND))
    key = jnp.where(to < OWN, to - i, 99)
    across = [ones(key == a - 2) for a in range(3)]
    unused, i, d = iotas((1, 10 * BAND))
    in_d = [ones((d >= 1 - b) & (d < BAND + 1 - b)) for b in range(3)]
    in_i = [ones((i >= 2 - a) & (i < OWN + 2 - a)) for a in range(3)]
    picks = []
    for a in range(3):
        for b in range(3):
            picks.append(along[a + b - 3] * (in_i[a] * in_d[b]))
            picks.append(across[a] * in_d[b])
    z = dot(jnp.concatenate(picks, axis=0), d0[...].reshape(10 * BAND, C)).astype(BF)
    z = jnp.concatenate([z[96 * k : 96 * k + 96] for k in range(9)], axis=1)
    own = jnp.concatenate([along[-1][:, BAND : 9 * BAND], across[1][:, BAND : 9 * BAND]], axis=0)
    top96 = dot(own, g1h[...].reshape(OWN * BAND, C)) + dot(own, g1l[...].reshape(OWN * BAND, C))
    top96 = top96 + dot_nt(z, side_by_side(w, 0))
    rcv[...] = jnp.zeros((128, C), F32)
    lcv[...] = jnp.zeros((64, C), F32)
    rcv[pl.ds(start, 72)] = top96[:72]
    lcv[pl.ds(start, OWN)] = top96[80:88]
    for j in range(4):
        for g in range(2):
            lanes = slice(HALF * g, HALF * g + HALF)
            out[4 * g + j, 0:16] = rcv[16 * j : 16 * j + 16, lanes].astype(BF)
            out[4 * g + j, 16:32] = rcv[64 + 16 * j : 80 + 16 * j, lanes].astype(BF)
            out[4 * g + j, 32:48] = lcv[16 * j : 16 * j + 16, lanes].astype(BF)
            out[4 * g + j, 48:64] = ccv[16 * j : 16 * j + 16].astype(BF)


def local_part(info, msg, w_own, w_z, w_s):
    vm = pltpu.VMEM
    scratch = [
        vm((27, C, C), BF),
        vm((176, C), F32),
        vm((176, C), F32),
        vm((192, HALF), F32),
        vm((48, C), F32),
        vm((112, C), F32),
        vm((40, C), F32),
        vm((2, 104, C), F32),
        vm((2, 40, C), F32),
        vm((2, 40, C), F32),
        vm((34, BAND, 3 * C), BF),
        vm((30, BAND, 3 * C), BF),
        vm((22, BAND, 3 * C), BF),
        vm((14, BAND, 3 * C), BF),
        vm((10, BAND, C), BF),
        vm((14, BAND, C), BF),
        vm((10, BAND, C), F32),
        vm((8, BAND, C), BF),
        vm((10, BAND, C), BF),
        vm((8, BAND, C), BF),
        vm((8, BAND, C), BF),
        vm((128, C), F32),
        vm((64, C), F32),
        vm((64, HALF), F32),
        pltpu.SemaphoreType.DMA((3, 3)),
    ]
    return pl.pallas_call(
        body,
        out_shape=jax.ShapeDtypeStruct((8, 64, HALF), BF),
        in_specs=[
            pl.BlockSpec(memory_space=pltpu.SMEM),
            pl.BlockSpec(memory_space=vm),
            pl.BlockSpec(memory_space=pl.ANY),
            pl.BlockSpec(memory_space=pl.ANY),
            pl.BlockSpec(memory_space=pl.ANY),
        ],
        out_specs=pl.BlockSpec(memory_space=vm),
        scratch_shapes=scratch,
        compiler_params=pltpu.CompilerParams(vmem_limit_bytes=48 * 2**20),
        cost_estimate=pl.CostEstimate(
            flops=6 * 10**9, bytes_accessed=5 * 10**6, transcendentals=2 * 10**6
        ),
        name="decoder",
    )(info, msg, w_own, w_z, w_s)


def z_pairs(chroms):
    pairs = []
    per_z = chroms // 4
    for ch in range(chroms):
        hi, rest = ch // per_z, ch % per_z
        for g in range(2):
            step = (1 if g == 0 else -1) * (1 if ch % 2 == 0 else -1)
            z = (2 * hi + g + step) % 8
            pairs.append((((z // 2) * per_z + rest) * 2 + z % 2, 2 * ch + g))
    return pairs


def copy_half(core, w_own, out, sem):
    moves = [
        pltpu.make_async_copy(
            w_own.at[pl.ds(3 * k, 3), pl.ds(pl.multiple_of(core[0] * HALF, HALF), HALF)],
            out.at[pl.ds(3 * k, 3)],
            sem.at[k],
        )
        for k in range(9)
    ]
    for move in moves:
        move.start()
    for move in moves:
        move.wait()


def own_part(core, w_own):
    return pl.pallas_call(
        copy_half,
        out_shape=pltpu.VMEM((27, HALF, HALF), BF),
        in_specs=[pl.BlockSpec(memory_space=pltpu.SMEM), pl.BlockSpec(memory_space=pl.ANY)],
        out_specs=pl.BlockSpec(memory_space=pltpu.VMEM),
        scratch_shapes=[pltpu.SemaphoreType.DMA((9,))],
        cost_estimate=pl.CostEstimate(flops=0, bytes_accessed=2 * 10**6, transcendentals=0),
        name="own_part",
    )(core, w_own)


def parts_of(x, count):
    parts = []
    for _ in range(count):
        hi = lax.reduce_precision(x, 8, 7)
        parts.append(hi.astype(BF))
        x = x - hi
    return parts


def local(left, right, weight, readout, cotangent):
    rows = left.shape[0]
    chroms = lax.axis_size(CHROM)
    slab = lax.axis_index(CHROM)
    core = lax.axis_index("core")
    chan = lax.axis_index("chan")
    own_w = weight.reshape(27, C, HALF)
    piece = own_part(core[None].astype(jnp.int32), own_w)
    piece, readout, cotangent = lax.optimization_barrier((piece, readout, cotangent))

    hi, lo = parts_of(cotangent, 2)
    read = jnp.pad(jnp.stack(parts_of(readout, 3)).reshape(6, BAND), ((0, rows - 6), (0, 0)))
    cot = jnp.concatenate([jnp.where(chan == 0, hi, lo), read], axis=1)
    mine = jnp.concatenate([left, right, cot], axis=0)
    piece, mine = lax.optimization_barrier((piece, mine))
    w_z = lax.ppermute(piece, "chan", [(0, 1), (1, 0)])
    slabs = 4
    groups = chroms // slabs
    next_group = [
        (slabs * (g + 1) + j, slabs * g + j) for g in range(groups - 1) for j in range(slabs)
    ]
    ends = [(slabs * g + 3, slabs * (g + 1) + 1) for g in range(groups - 1)]
    ends += [(slabs * (g + 2), slabs * g + 3) for g in range(groups - 2)]
    after = lax.ppermute(mine, CHROM, next_group)
    edge = lax.ppermute(mine, CHROM, ends)
    extra = jnp.where(slab % slabs == 0, after, edge)
    block = jnp.concatenate([mine, after[rows : 2 * rows], extra], axis=0)
    msg = lax.all_to_all(
        jnp.broadcast_to(block[None], (8,) + block.shape), GROUP, 0, 0, tiled=False
    )
    msg, w_z = lax.optimization_barrier((msg, w_z))
    w_s = lax.ppermute(w_z, "core", [(0, 1), (1, 0)])
    q = lax.axis_index(("yl", "core", "chan"))
    info = jnp.stack(
        [q, rows * slab + OWN * chan, core, chan, rows * chroms]
    ).astype(jnp.int32)
    sent = local_part(info, msg, own_w, w_z, w_s)
    got = jnp.sum(lax.all_to_all(sent, GROUP, 0, 0, tiled=False).astype(F32), axis=0)
    moved = lax.ppermute(got[16:32], CHROM, [(b, a) for a, b in next_group])
    return got[48:64, :BAND] + got[48:64, BAND:], got[32:48], got[0:16] + moved


def solution(mesh):
    chroms = mesh.shape["chrom"]
    small = Mesh(
        mesh.devices.reshape(chroms // 16, 4, 2, 2, 2), ("h", "yh", "yl", "core", "chan")
    )
    return jax.shard_map(
        local,
        mesh=small,
        in_specs=(
            P(CHROM, "chan"),
            P(CHROM, "chan"),
            P(None, None, None, None, "chan"),
            P("chan"),
            P(CHROM, None),
        ),
        out_specs=(P(CHROM, None), P(CHROM, "chan"), P(CHROM, "chan")),
        check_vma=False,
    )
```
